32 devices in a mesh: groups: 2 (over y), label: 4 (over x, core), dp: 4 (over z).
Axes of the slice: x: 2, y: 2, z: 4, core: 2. Of those that a mesh axis runs over, the one named last changes fastest.
Arguments:
- embeds: bfloat16 [24576, 1024], P(('groups', 'label', 'dp')), parts along dimension 0, may hold values from -6 to 6
- weights: bfloat16 [2048, 1024], P(('label', 'dp')), may hold values from -0.1875 to 0.1875
- pos_ids: int32 [24576, 8], P(('groups', 'label', 'dp')), parts along dimension 0, may hold values from 0 to 2047, as said below
- pos_count: int32 [24576], P(('groups', 'label', 'dp')), parts along dimension 0, may hold values from 1 to 8
Outputs:
- grad_weight: bfloat16 [4096, 1024], P(('groups', 'label', 'dp')), parts along dimension 0
- grad_embed: bfloat16 [24576, 1024], P(('groups', 'label', 'dp')), parts along dimension 0
The draws below stay inside these ranges and needn't reach their ends.
There are 2 independent parts, one for each index of `groups`. The reference program is written for one: setup_inputs(seed, part) draws one part's arguments, and reference() takes and returns one part's arrays. A program takes and returns all parts, laid end to end along the dimension named above; an argument that names none is the same for every part. Nothing has to cross between parts.
Inputs may be any that keep to these rules, and one draw needn't show every extreme that they name: `pos_ids`: entry p of a row lies in [p * 256, (p + 1) * 256), so a row's entries are distinct.
All inputs are finite; a program needn't handle non-finite values.
Results may differ from the reference program's by a relative error of at most 0.012.
Values may be sent and summed in bfloat16 or wider, within the bound.
No kernel may reach another device: no remote copies, remote signals or barrier semaphores. Data moves between devices by JAX's collectives and lax.ppermute only.
A program may use at most 64 MiB of HBM per device.

```python
import jax
import jax.numpy as jnp
from jax import lax

D = 1024
STRETCH = 512
POS = 8
STEPS = 2
B_DEV = 768
GROUP_ROWS = 3072
ROWS = 12288
LABELS = 2048
N_LABEL = 4
N_DP = 4


def draw_pos_ids(key, part):
    key = jax.random.fold_in(key, 11)
    span = LABELS // POS
    offsets = jax.random.randint(key, (ROWS, POS), 0, span, dtype=jnp.int32)
    starts = jnp.arange(POS, dtype=jnp.int32)[None, :] * span
    values = starts + offsets
    values = values.at[0, 0].set(0)
    values = values.at[0, POS - 1].set(LABELS - 1)
    return values


def draw_pos_count(key, part):
    key = jax.random.fold_in(key, 23)
    counts = jax.random.randint(key, (ROWS,), 1, POS + 1, dtype=jnp.int32)
    counts = counts.at[0].set(POS)
    counts = counts.at[1].set(1)
    return counts


def block_scale(own_key, shape, split, low, largest):
    loudness, own = 1.0, jax.random.fold_in(own_key, 6)
    for axis_at, shards_of in split:
        steps = jnp.exp(jax.random.uniform(jax.random.fold_in(own, axis_at), (shards_of,), jnp.float32, low / len(split), largest / len(split)))
        loudness = loudness * jnp.repeat(steps, shape[axis_at] // shards_of).reshape([-1 if axis == axis_at else 1 for axis in range(len(shape))])
    return loudness


def noise(rng, extent, spread, reach, pieces=(), kind=jnp.bfloat16):
    result = jax.random.normal(rng, extent, jnp.float32) * spread
    if len(pieces) > 0:
        result = block_scale(rng, extent, pieces, -0.22, 0.18) * result
    return jnp.clip(result, min=-reach, max=reach).astype(kind)


def setup_inputs(seed: int = 0, part: int = 0) -> dict:
    arg_keys = jax.random.split(jax.random.key(seed), 5)
    part_keys = jax.random.split(jax.random.fold_in(arg_keys[4], part), 5)
    return {
        "embeds": noise(part_keys[0], (ROWS, D), 1.0, 6.0, ((0, 16),)),
        "weights": noise(arg_keys[1], (LABELS, D), D ** -0.5, 0.1875, ((0, 16),)),
        "pos_ids": draw_pos_ids(jax.random.fold_in(jax.random.fold_in(arg_keys[4], part), 71), part),
        "pos_count": draw_pos_count(jax.random.fold_in(jax.random.fold_in(arg_keys[4], part), 71), part),
    }


def reference(embeds, weights, pos_ids, pos_count):
    rows = embeds.reshape(N_LABEL, GROUP_ROWS, D)
    stretches = weights.reshape(N_LABEL, STRETCH, D)
    ids = pos_ids.reshape(N_LABEL, GROUP_ROWS, POS)
    counts = pos_count.reshape(N_LABEL, GROUP_ROWS)
    blocks = jnp.arange(N_LABEL, dtype=jnp.int32)
    scale = 1.0 / (GROUP_ROWS ** 0.5)
    grad_x = jnp.zeros((N_LABEL, GROUP_ROWS, D), jnp.float32)
    grad_w = jnp.zeros((N_LABEL, STRETCH, D), jnp.float32)
    for step in range(STEPS):
        visited = jnp.roll(stretches, step, axis=0)

        def one_block(item):
            row_blk, stretch_blk, id_blk, count_blk, block = item
            owner = (block - step) % N_LABEL
            labels = owner * STRETCH + jnp.arange(STRETCH, dtype=jnp.int32)
            valid = jnp.arange(POS, dtype=jnp.int32)[None, :] < count_blk[:, None]
            hits = (id_blk[:, :, None] == labels[None, None, :]) & valid[:, :, None]
            target = jnp.any(hits, axis=1).astype(jnp.float32)
            logits = jnp.dot(row_blk, stretch_blk.T, preferred_element_type=jnp.float32)
            delta = (jax.nn.sigmoid(logits) - target).astype(jnp.bfloat16)
            gx = jnp.dot(delta, stretch_blk, preferred_element_type=jnp.float32)
            runs_d = delta.reshape(N_DP, B_DEV, STRETCH).astype(jnp.float32)
            runs_x = row_blk.reshape(N_DP, B_DEV, D).astype(jnp.float32)
            terms = (jnp.einsum("nbc,nbd->ncd", runs_d, runs_x) * scale).astype(jnp.bfloat16)
            return gx, jnp.sum(terms.astype(jnp.float32), axis=0)

        gx, parts = lax.map(one_block, (rows, visited, ids, counts, blocks))
        grad_x = grad_x + gx
        grad_w = grad_w + jnp.roll(parts, -step, axis=0)
    return grad_w.reshape(LABELS, D).astype(jnp.bfloat16), grad_x.reshape(ROWS, D).astype(jnp.bfloat16)
```

```python
import math

import jax
import jax.numpy as jnp
from jax import lax
from jax.sharding import PartitionSpec as P


def local(embeds, weights, pos_ids, pos_count):
    n_label = lax.axis_size("label")
    n_dp = lax.axis_size("dp")
    me_label = lax.axis_index("label")
    me_dp = lax.axis_index("dp")
    rows_dev, width = embeds.shape
    ch_dev = weights.shape[0]
    stretch = ch_dev * n_dp
    slots = pos_ids.shape[1]
    span = stretch * n_label // slots
    scale = 1.0 / math.sqrt(rows_dev * n_dp)
    valid = jnp.arange(slots, dtype=jnp.int32)[None, :] < pos_count[:, None]
    ids = jnp.where(valid, pos_ids, -1)

    def to_dp(x, k):
        return lax.ppermute(x, "dp", [(i, i ^ k) for i in range(n_dp)])

    def to_label(x, by):
        return lax.ppermute(x, "label", [(i, (i + by) % n_label) for i in range(n_label)])

    def delta_of(piece, owner, k):
        start = owner * stretch + (me_dp ^ k) * ch_dev
        column = lax.dynamic_slice_in_dim(ids, start // span, 1, axis=1)
        labels = start + jnp.arange(ch_dev, dtype=jnp.int32)
        target = (column == labels[None, :]).astype(jnp.float32)
        logits = lax.dot_general(
            embeds, piece, (((1,), (1,)), ((), ())), preferred_element_type=jnp.float32
        )
        return (jax.nn.sigmoid(logits) - target).astype(jnp.bfloat16)

    def grad_w_of(delta):
        return lax.dot_general(
            delta, embeds, (((0,), (0,)), ((), ())), preferred_element_type=jnp.float32
        ) * scale

    order = list(range(n_dp))
    prev_owner = (me_label - 1) % n_label
    own = [weights if k == 0 else to_dp(weights, k) for k in order]
    prev = [to_label(own[k], 1) for k in order]
    d_own = [delta_of(own[k], me_label, k) for k in order]
    d_prev = [delta_of(prev[k], prev_owner, k) for k in order]
    back = [to_label(grad_w_of(d_prev[k]).astype(jnp.bfloat16), -1) for k in order]
    total = [grad_w_of(d_own[k]) + back[k].astype(jnp.float32) for k in order]
    grad_w = total[0]
    for k in order[1:]:
        grad_w = grad_w + to_dp(total[k].astype(jnp.bfloat16), k).astype(jnp.float32)
    grad_x = jnp.dot(
        jnp.concatenate(d_own + d_prev, axis=1),
        jnp.concatenate(own + prev, axis=0),
        preferred_element_type=jnp.float32,
    )
    return (grad_w.astype(jnp.bfloat16), grad_x.astype(jnp.bfloat16))


def solution(mesh):
    return jax.shard_map(
        local,
        mesh=mesh,
        in_specs=(
            P(("groups", "label", "dp"), None),
            P(("label", "dp"), None),
            P(("groups", "label", "dp"), None),
            P(("groups", "label", "dp")),
        ),
        out_specs=(P(("groups", "label", "dp"), None), P(("groups", "label", "dp"), None)),
        check_vma=False,
    )
```

```python
import math

import jax
import jax.numpy as jnp
from jax import lax
from jax.sharding import PartitionSpec as P


def local(embeds, weights, pos_ids, pos_count):
    n_label = lax.axis_size("label")
    n_dp = lax.axis_size("dp")
    me_label = lax.axis_index("label")
    me_dp = lax.axis_index("dp")
    rows_dev, width = embeds.shape
    ch_dev = weights.shape[0]
    stretch = ch_dev * n_dp
    slots = pos_ids.shape[1]
    span = stretch * n_label // slots
    scale = 1.0 / math.sqrt(rows_dev * n_dp)
    valid = jnp.arange(slots, dtype=jnp.int32)[None, :] < pos_count[:, None]
    ids = jnp.where(valid, pos_ids, -1)

    def to_dp(x, k):
        return lax.ppermute(x, "dp", [(i, i ^ k) for i in range(n_dp)])

    def to_label(x, by):
        return lax.ppermute(x, "label", [(i, (i + by) % n_label) for i in range(n_label)])

    def delta_of(piece, owner, k):
        start = owner * stretch + (me_dp ^ k) * ch_dev
        column = lax.dynamic_slice_in_dim(ids, start // span, 1, axis=1)
        labels = start + jnp.arange(ch_dev, dtype=jnp.int32)
        target = (column == labels[None, :]).astype(jnp.float32)
        logits = lax.dot_general(
            embeds, piece, (((1,), (1,)), ((), ())), preferred_element_type=jnp.float32
        )
        return (jax.nn.sigmoid(logits) - target).astype(jnp.bfloat16)

    def grad_w_of(delta):
        return lax.dot_general(
            delta, embeds, (((0,), (0,)), ((), ())), preferred_element_type=jnp.float32
        ) * scale

    prev_owner = (me_label - 1) % n_label
    last = [embeds]

    def in_turn(x):
        x, _ = lax.optimization_barrier((x, last[0]))
        return x

    def score(piece, owner, k):
        delta = delta_of(in_turn(piece), owner, k)
        last[0] = grad_w_of(delta).astype(jnp.bfloat16)
        return delta, last[0]

    def join(k):
        last[0] = (in_turn(w_own[k]).astype(jnp.float32) + in_turn(back[k]).astype(jnp.float32)).astype(jnp.bfloat16)
        return last[0]

    d_own, w_own, d_prev, w_prev, prev, back, moved = {}, {}, {}, {}, {}, {}, {}
    own = [weights if k == 0 else to_dp(weights, k) for k in range(n_dp)]
    for k in range(n_dp):
        own[k] = in_turn(own[k])
        prev[k] = to_label(own[k], 1)
        d_own[k], w_own[k] = score(own[k], me_label, k)
        if k > 1:
            moved[k - 1] = to_dp(join(k - 1), k - 1)
        d_prev[k], w_prev[k] = score(prev[k], prev_owner, k)
        if k > 0:
            back[k] = to_label(w_prev[k], -1)
    stacked = jnp.concatenate(list(d_own.values()) + list(d_prev.values()), axis=1)
    grad_x = jnp.dot(
        in_turn(stacked), jnp.concatenate(own + list(prev.values()), axis=0), preferred_element_type=jnp.float32
    ).astype(jnp.bfloat16)
    last[0] = grad_x
    back[0] = to_label(in_turn(w_prev[0]), -1)
    if n_dp > 1:
        moved[n_dp - 1] = to_dp(join(n_dp - 1), n_dp - 1)
    grad_w = w_own[0].astype(jnp.float32) + in_turn(back[0]).astype(jnp.float32)
    for k in range(1, n_dp):
        grad_w = grad_w + in_turn(moved[k]).astype(jnp.float32)
    return (grad_w.astype(jnp.bfloat16), grad_x)


def solution(mesh):
    return jax.shard_map(
        local,
        mesh=mesh,
        in_specs=(
            P(("groups", "label", "dp"), None),
            P(("label", "dp"), None),
            P(("groups", "label", "dp"), None),
            P(("groups", "label", "dp")),
        ),
        out_specs=(P(("groups", "label", "dp"), None), P(("groups", "label", "dp"), None)),
        check_vma=False,
    )
```

```python
import math

import jax
import jax.numpy as jnp
from jax import lax
from jax.sharding import PartitionSpec as P


def local(embeds, weights, pos_ids, pos_count):
    n_groups = lax.axis_size("groups")
    n_label = lax.axis_size("label")
    n_dp = lax.axis_size("dp")
    me_group = lax.axis_index("groups")
    me_label = lax.axis_index("label")
    me_dp = lax.axis_index("dp")
    rows_dev, width = embeds.shape
    ch_dev = weights.shape[0]
    stretch = ch_dev * n_dp
    half = ch_dev // 2
    slots = pos_ids.shape[1]
    span = stretch * n_label // slots
    scale = 1.0 / math.sqrt(rows_dev * n_dp)
    even = me_label % 2 == 0
    valid = jnp.arange(slots, dtype=jnp.int32)[None, :] < pos_count[:, None]
    ids = jnp.where(valid, pos_ids, -1)
    last = [embeds]

    def in_turn(x):
        x, _ = lax.optimization_barrier((x, last[0]))
        return x

    def to_dp(x, k):
        return lax.ppermute(x, "dp", [(i, i ^ k) for i in range(n_dp)])

    def to_dp_of(parity, x, k):
        pairs = [
            (label * n_dp + i, label * n_dp + (i ^ k))
            for label in range(parity, n_label, 2) for i in range(n_dp)
        ]
        return lax.ppermute(x, ("label", "dp"), pairs)

    def to_group(x):
        return lax.ppermute(x, "groups", [(i, i ^ 1) for i in range(n_groups)])

    def to_label(parity, x, by):
        return lax.ppermute(x, "label", [(i, (i + by) % n_label) for i in range(parity, n_label, 2)])

    def delta_of(piece, owner, k):
        start = owner * stretch + (me_dp ^ k) * ch_dev
        column = lax.dynamic_slice_in_dim(ids, start // span, 1, axis=1)
        labels = start + jnp.arange(ch_dev, dtype=jnp.int32)
        target = (column == labels[None, :]).astype(jnp.float32)
        logits = lax.dot_general(
            embeds, piece, (((1,), (1,)), ((), ())), preferred_element_type=jnp.float32
        )
        return (jax.nn.sigmoid(logits) - target).astype(jnp.bfloat16)

    def score(piece, owner, k):
        delta = delta_of(in_turn(piece), owner, k)
        last[0] = (
            lax.dot_general(delta, embeds, (((0,), (0,)), ((), ())), preferred_element_type=jnp.float32) * scale
        ).astype(jnp.bfloat16)
        return delta, last[0]

    def join(mine, theirs):
        last[0] = (in_turn(mine).astype(jnp.float32) + in_turn(theirs).astype(jnp.float32)).astype(jnp.bfloat16)
        return last[0]

    near = jnp.where(even, me_label, me_label - 1)
    far = jnp.where(even, (me_label - 1) % n_label, me_label)
    w_near, w_far, d_near, d_far, g_near, g_far = {}, {}, {}, {}, {}, {}
    back_near, back_far, sum_near, sum_far, moved_near, moved_far = {}, {}, {}, {}, {}, {}
    passed_near, passed_far, pieces = {}, {}, {0: weights}

    def pass_on(k):
        pieces[k] = in_turn(pieces[k])
        passed_near[k] = to_label(0, pieces[k], 1)
        passed_far[k] = to_label(1, pieces[k], 1)

    def near_step(k):
        w_near[k] = jnp.where(even, pieces[k], passed_near[k])
        d_near[k], g_near[k] = score(w_near[k], near, k)
        back_near[k] = to_label(1, g_near[k], -1)

    def far_step(k):
        w_far[k] = jnp.where(even, in_turn(passed_far[k]), pieces[k])
        d_far[k], g_far[k] = score(w_far[k], far, k)
        back_far[k] = to_label(0, g_far[k], -1)

    def near_send(k):
        sum_near[k] = join(g_near[k], back_near[k])
        if k > 0:
            moved_near[k] = to_dp_of(0, sum_near[k], k)

    def far_send(k):
        sum_far[k] = join(g_far[k], back_far[k])
        if k > 0:
            moved_far[k] = to_dp_of(1, sum_far[k], k)

    mine = lax.dynamic_slice_in_dim(weights, me_group * half, half, axis=0)
    halves = {k: to_dp(mine, k) for k in range(2, n_dp)}
    others = {}
    pieces[1] = to_dp(weights, 1)

    def swap(k):
        halves[k] = in_turn(halves[k])
        others[k] = to_group(halves[k])

    def whole(k):
        other = in_turn(others[k])
        pieces[k] = jnp.where(
            me_group == 0,
            jnp.concatenate([halves[k], other], axis=0),
            jnp.concatenate([other, halves[k]], axis=0),
        )

    pass_on(0)
    near_step(0)
    far_step(0)
    pass_on(1)
    near_step(1)
    swap(2)
    near_send(1)
    far_step(1)
    for k in range(2, n_dp):
        if k + 1 < n_dp:
            swap(k + 1)
        whole(k)
        pass_on(k)
        near_step(k)
        near_send(k)
        if k == 2:
            far_send(1)
        if k > 2:
            far_step(k - 1)
    far_step(n_dp - 1)
    order = range(n_dp)
    grad_x = jnp.dot(
        in_turn(jnp.concatenate([d_near[k] for k in order] + [d_far[k] for k in order], axis=1)),
        jnp.concatenate([w_near[k] for k in order] + [w_far[k] for k in order], axis=0),
        preferred_element_type=jnp.float32,
    ).astype(jnp.bfloat16)
    last[0] = grad_x
    for k in range(2, n_dp):
        far_send(k)
    near_send(0)
    far_send(0)
    grad_w = jnp.where(even, sum_near[0], sum_far[0]).astype(jnp.float32)
    for k in range(1, n_dp):
        grad_w = grad_w + jnp.where(even, in_turn(moved_near[k]), in_turn(moved_far[k])).astype(jnp.float32)
    return (grad_w.astype(jnp.bfloat16), grad_x)


def solution(mesh):
    return jax.shard_map(
        local,
        mesh=mesh,
        in_specs=(
            P(("groups", "label", "dp"), None),
            P(("label", "dp"), None),
            P(("groups", "label", "dp"), None),
            P(("groups", "label", "dp")),
        ),
        out_specs=(P(("groups", "label", "dp"), None), P(("groups", "label", "dp"), None)),
        check_vma=False,
    )
```

```python
import math

import jax
import jax.numpy as jnp
from jax import lax
from jax.sharding import PartitionSpec as P


def local(embeds, weights, pos_ids, pos_count):
    n_label = lax.axis_size("label")
    n_dp = lax.axis_size("dp")
    me_label = lax.axis_index("label")
    me_dp = lax.axis_index("dp")
    rows_dev, width = embeds.shape
    ch_dev = weights.shape[0]
    stretch = ch_dev * n_dp
    slots = pos_ids.shape[1]
    span = stretch * n_label // slots
    scale = 1.0 / math.sqrt(rows_dev * n_dp)
    valid = jnp.arange(slots, dtype=jnp.int32)[None, :] < pos_count[:, None]
    ids = jnp.where(valid, pos_ids, -1)
    last = [embeds]

    def in_turn(x):
        x, _ = lax.optimization_barrier((x, last[0]))
        return x

    def to_dp(x, k):
        return lax.ppermute(x, "dp", [(i, i ^ k) for i in range(n_dp)])

    def to_label(x, by):
        return lax.ppermute(x, "label", [(i, (i + by) % n_label) for i in range(n_label)])

    def delta_of(rows, row_ids, piece, k):
        start = me_label * stretch + (me_dp ^ k) * ch_dev
        column = lax.dynamic_slice_in_dim(row_ids, start // span, 1, axis=1)
        labels = start + jnp.arange(ch_dev, dtype=jnp.int32)
        target = (column == labels[None, :]).astype(jnp.float32)
        logits = lax.dot_general(
            rows, piece, (((1,), (1,)), ((), ())), preferred_element_type=jnp.float32
        )
        return (jax.nn.sigmoid(logits) - target).astype(jnp.bfloat16)

    def grad_w_of(delta, rows):
        return lax.dot_general(
            delta, rows, (((0,), (0,)), ((), ())), preferred_element_type=jnp.float32
        )

    def grad_x_of(deltas):
        return jnp.dot(
            in_turn(jnp.concatenate([deltas[k] for k in range(n_dp)], axis=1)),
            jnp.concatenate([pieces[k] for k in range(n_dp)], axis=0),
            preferred_element_type=jnp.float32,
        )

    d_own, d_next, g_own, total, moved = {}, {}, {}, {}, {}
    pieces = {k: weights if k == 0 else to_dp(weights, k) for k in range(n_dp)}
    next_rows = to_label(embeds, -1)
    next_ids = to_label(ids, -1)

    def own_step(k):
        pieces[k] = in_turn(pieces[k])
        d_own[k] = delta_of(embeds, ids, pieces[k], k)
        g_own[k] = grad_w_of(d_own[k], embeds)
        last[0] = g_own[k]

    def next_step(k):
        d_next[k] = delta_of(next_rows, next_ids, in_turn(pieces[k]), k)
        total[k] = (g_own[k] + grad_w_of(d_next[k], next_rows)) * scale
        if k > 0:
            total[k] = total[k].astype(jnp.bfloat16)
            moved[k] = to_dp(total[k], k)
        last[0] = total[k]

    own_step(0)
    for k in range(1, n_dp - 1):
        own_step(k)
    for k in range(n_dp - 2, 0, -1):
        next_step(k)
    next_step(0)
    if n_dp > 1:
        own_step(n_dp - 1)
        next_step(n_dp - 1)
    theirs = grad_x_of(d_next).astype(jnp.bfloat16)
    last[0] = theirs
    back = to_label(theirs, 1)
    grad_x = grad_x_of(d_own)
    last[0] = grad_x
    grad_x = (grad_x + in_turn(back).astype(jnp.float32)).astype(jnp.bfloat16)
    last[0] = grad_x
    grad_w = total[0]
    for k in range(1, n_dp):
        grad_w = grad_w + in_turn(moved[k]).astype(jnp.float32)
    return (grad_w.astype(jnp.bfloat16), grad_x)


def solution(mesh):
    return jax.shard_map(
        local,
        mesh=mesh,
        in_specs=(
            P(("groups", "label", "dp"), None),
            P(("label", "dp"), None),
            P(("groups", "label", "dp"), None),
            P(("groups", "label", "dp")),
        ),
        out_specs=(P(("groups", "label", "dp"), None), P(("groups", "label", "dp"), None)),
        check_vma=False,
    )
```

```python
import math

import jax
import jax.numpy as jnp
from jax import lax
from jax.sharding import PartitionSpec as P


def local(embeds, weights, pos_ids, pos_count):
    n_label = lax.axis_size("label")
    n_dp = lax.axis_size("dp")
    me_label = lax.axis_index("label")
    me_dp = lax.axis_index("dp")
    rows_dev, width = embeds.shape
    ch_dev = weights.shape[0]
    stretch = ch_dev * n_dp
    slots = pos_ids.shape[1]
    span = stretch * n_label // slots
    scale = 1.0 / math.sqrt(rows_dev * n_dp)
    valid = jnp.arange(slots, dtype=jnp.int32)[None, :] < pos_count[:, None]
    ids = jnp.where(valid, pos_ids, -1)
    last = [embeds]

    def in_turn(x):
        x, _ = lax.optimization_barrier((x, last[0]))
        return x

    def to_dp(x, k):
        return lax.ppermute(x, "dp", [(i, i ^ k) for i in range(n_dp)])

    def to_label(x, by):
        return lax.ppermute(x, "label", [(i, (i + by) % n_label) for i in range(n_label)])

    def delta_of(rows, row_ids, piece, k):
        start = me_label * stretch + (me_dp ^ k) * ch_dev
        column = lax.dynamic_slice_in_dim(row_ids, start // span, 1, axis=1)
        labels = start + jnp.arange(ch_dev, dtype=jnp.int32)
        target = (column == labels[None, :]).astype(jnp.float32)
        logits = lax.dot_general(
            rows, piece, (((1,), (1,)), ((), ())), preferred_element_type=jnp.float32
        )
        return (jax.nn.sigmoid(logits) - target).astype(jnp.bfloat16)

    def grad_w_of(delta, rows):
        return lax.dot_general(
            delta, rows, (((0,), (0,)), ((), ())), preferred_element_type=jnp.float32
        )

    def grad_x_of(deltas):
        return jnp.dot(
            in_turn(jnp.concatenate([deltas[k] for k in range(n_dp)], axis=1)),
            jnp.concatenate([pieces[k] for k in range(n_dp)], axis=0),
            preferred_element_type=jnp.float32,
        )

    d_own, d_next, g_own, total, moved = {}, {}, {}, {}, {}
    pieces = {0: weights}
    for k in range(1, n_dp):
        step = k & -k
        pieces[k] = to_dp(pieces[k ^ step], step)
    next_rows = to_label(embeds, -1)

    def own_step(k):
        pieces[k] = in_turn(pieces[k])
        d_own[k] = delta_of(embeds, ids, pieces[k], k)
        g_own[k] = grad_w_of(d_own[k], embeds)
        last[0] = g_own[k]

    def next_step(k):
        d_next[k] = delta_of(next_rows, next_ids, in_turn(pieces[k]), k)
        total[k] = (g_own[k] + grad_w_of(d_next[k], next_rows)) * scale
        if k > 0:
            total[k] = total[k].astype(jnp.bfloat16)
            moved[k] = to_dp(total[k], k)
        last[0] = total[k]

    own_step(0)
    next_ids = to_label(in_turn(ids), -1)
    for k in range(1, n_dp - 1):
        own_step(k)
    for k in range(n_dp - 1):
        next_step(k)
    if n_dp > 1:
        own_step(n_dp - 1)
        next_step(n_dp - 1)
    theirs = grad_x_of(d_next).astype(jnp.bfloat16)
    last[0] = theirs
    back = to_label(theirs, 1)
    grad_x = grad_x_of(d_own)
    last[0] = grad_x
    grad_x = (grad_x + in_turn(back).astype(jnp.float32)).astype(jnp.bfloat16)
    last[0] = grad_x
    grad_w = total[0]
    for k in range(1, n_dp):
        grad_w = grad_w + in_turn(moved[k]).astype(jnp.float32)
    return (grad_w.astype(jnp.bfloat16), grad_x)


def solution(mesh):
    return jax.shard_map(
        local,
        mesh=mesh,
        in_specs=(
            P(("groups", "label", "dp"), None),
            P(("label", "dp"), None),
            P(("groups", "label", "dp"), None),
            P(("groups", "label", "dp")),
        ),
        out_specs=(P(("groups", "label", "dp"), None), P(("groups", "label", "dp"), None)),
        check_vma=False,
    )
```

```python
import math

import jax
import jax.numpy as jnp
from jax import lax
from jax.sharding import PartitionSpec as P


def local(embeds, weights, pos_ids, pos_count):
    n_label = lax.axis_size("label")
    n_dp = lax.axis_size("dp")
    me_label = lax.axis_index("label")
    me_dp = lax.axis_index("dp")
    rows_dev, width = embeds.shape
    ch_dev = weights.shape[0]
    stretch = ch_dev * n_dp
    slots = pos_ids.shape[1]
    span = stretch * n_label // slots
    scale = 1.0 / math.sqrt(rows_dev * n_dp)
    valid = jnp.arange(slots, dtype=jnp.int32)[None, :] < pos_count[:, None]
    ids = jnp.where(valid, pos_ids, -1)
    last = [embeds]

    def in_turn(x):
        x, _ = lax.optimization_barrier((x, last[0]))
        return x

    def to_dp(x, k):
        return lax.ppermute(x, "dp", [(i, i ^ k) for i in range(n_dp)])

    def to_label(x, by):
        return lax.ppermute(x, "label", [(i, (i + by) % n_label) for i in range(n_label)])

    def delta_of(rows, row_ids, piece, k):
        start = me_label * stretch + (me_dp ^ k) * ch_dev
        column = lax.dynamic_slice_in_dim(row_ids, start // span, 1, axis=1)
        labels = start + jnp.arange(ch_dev, dtype=jnp.int32)
        target = (column == labels[None, :]).astype(jnp.float32)
        logits = lax.dot_general(
            rows, piece, (((1,), (1,)), ((), ())), preferred_element_type=jnp.float32
        )
        return (jax.nn.sigmoid(logits) - target).astype(jnp.bfloat16)

    def grad_w_of(delta, rows):
        return lax.dot_general(
            delta, rows, (((0,), (0,)), ((), ())), preferred_element_type=jnp.float32
        )

    def grad_x_of(deltas):
        return jnp.dot(
            in_turn(jnp.concatenate([deltas[k] for k in range(n_dp)], axis=1)),
            jnp.concatenate([pieces[k] for k in range(n_dp)], axis=0),
            preferred_element_type=jnp.float32,
        )

    d_own, d_next, g_own, total, moved = {}, {}, {}, {}, {}
    pieces = {0: weights}
    for k in range(1, n_dp):
        step = k & -k
        pieces[k] = to_dp(pieces[k ^ step], step)
    next_rows = to_label(embeds, -1)

    def own_step(k):
        pieces[k] = in_turn(pieces[k])
        d_own[k] = delta_of(embeds, ids, pieces[k], k)
        g_own[k] = grad_w_of(d_own[k], embeds)
        last[0] = g_own[k]

    def next_step(k):
        d_next[k] = delta_of(next_rows, next_ids, in_turn(pieces[k]), k)
        total[k] = (g_own[k] + grad_w_of(d_next[k], next_rows)) * scale
        if k > 0:
            total[k] = total[k].astype(jnp.bfloat16)
            moved[k] = to_dp(total[k], k)
        last[0] = total[k]

    own_step(0)
    next_ids = to_label(in_turn(ids), -1)
    for k in range(1, n_dp - 1):
        own_step(k)
    next_ids = in_turn(next_ids)
    for k in range(n_dp - 1):
        next_step(k)
    if n_dp > 1:
        own_step(n_dp - 1)
        next_step(n_dp - 1)
    theirs = grad_x_of(d_next).astype(jnp.bfloat16)
    last[0] = theirs
    back = to_label(theirs, 1)
    grad_x = grad_x_of(d_own)
    last[0] = grad_x
    grad_x = (grad_x + in_turn(back).astype(jnp.float32)).astype(jnp.bfloat16)
    last[0] = grad_x
    grad_w = total[0]
    for k in range(1, n_dp):
        grad_w = grad_w + in_turn(moved[k]).astype(jnp.float32)
    return (grad_w.astype(jnp.bfloat16), grad_x)


def solution(mesh):
    return jax.shard_map(
        local,
        mesh=mesh,
        in_specs=(
            P(("groups", "label", "dp"), None),
            P(("label", "dp"), None),
            P(("groups", "label", "dp"), None),
            P(("groups", "label", "dp")),
        ),
        out_specs=(P(("groups", "label", "dp"), None), P(("groups", "label", "dp"), None)),
        check_vma=False,
    )
```

```python
import math

import jax
import jax.numpy as jnp
from jax import lax
from jax.sharding import PartitionSpec as P

CHUNKS = 1
DIRECT_EIGHTHS = 2


def local(embeds, weights, pos_ids, pos_count):
    n_label = lax.axis_size("label")
    n_dp = lax.axis_size("dp")
    me_label = lax.axis_index("label")
    me_dp = lax.axis_index("dp")
    rows_dev, width = embeds.shape
    ch_dev = weights.shape[0]
    stretch = ch_dev * n_dp
    slots = pos_ids.shape[1]
    span = stretch * n_label // slots
    scale = 1.0 / math.sqrt(rows_dev * n_dp)
    run = rows_dev // CHUNKS
    direct = ch_dev * DIRECT_EIGHTHS // 8
    valid = jnp.arange(slots, dtype=jnp.int32)[None, :] < pos_count[:, None]
    ids = jnp.where(valid, pos_ids, -1)
    last = [embeds]

    def in_turn(x):
        x, _ = lax.optimization_barrier((x, last[0]))
        return x

    def to_dp(x, k):
        return lax.ppermute(x, "dp", [(i, i ^ k) for i in range(n_dp)])

    def to_label(x, by):
        return lax.ppermute(x, "label", [(i, (i + by) % n_label) for i in range(n_label)])

    def delta_of(rows, row_ids, piece, k):
        start = me_label * stretch + (me_dp ^ k) * ch_dev
        column = lax.dynamic_slice_in_dim(row_ids, start // span, 1, axis=1)
        labels = start + jnp.arange(ch_dev, dtype=jnp.int32)
        target = (column == labels[None, :]).astype(jnp.float32)
        logits = lax.dot_general(
            rows, piece, (((1,), (1,)), ((), ())), preferred_element_type=jnp.float32
        )
        return (jax.nn.sigmoid(logits) - target).astype(jnp.bfloat16)

    def grad_w_of(delta, rows):
        return lax.dot_general(
            delta, rows, (((0,), (0,)), ((), ())), preferred_element_type=jnp.float32
        )

    def grad_x_of(deltas):
        return jnp.dot(
            in_turn(jnp.concatenate(deltas, axis=1)),
            jnp.concatenate([pieces[k] for k in range(n_dp)], axis=0),
            preferred_element_type=jnp.float32,
        )

    pieces = {0: weights}
    for k in range(1, n_dp):
        step = k & -k
        pieces[k] = to_dp(pieces[k ^ step], step)
    next_rows = [to_label(embeds[c * run:(c + 1) * run], -1) for c in range(CHUNKS)]
    d_own, g_own = {}, {}
    d_next = [{} for _ in range(CHUNKS)]

    def own_step(k):
        pieces[k] = in_turn(pieces[k])
        d_own[k] = delta_of(embeds, ids, pieces[k], k)
        g_own[k] = grad_w_of(d_own[k], embeds)
        last[0] = g_own[k]

    def next_step(c, k):
        d_next[c][k] = delta_of(next_rows[c], next_ids[c * run:(c + 1) * run], in_turn(pieces[k]), k)
        g_own[k] = g_own[k] + grad_w_of(d_next[c][k], next_rows[c])
        last[0] = g_own[k]

    own_step(0)
    next_ids = to_label(in_turn(ids), -1)
    for k in range(1, n_dp):
        own_step(k)
    next_ids = in_turn(next_ids)
    for c in range(CHUNKS):
        for k in range(n_dp - 1, -1, -1):
            next_step(c, k)
    theirs = [grad_x_of([d_next[c][k] for k in range(n_dp)]).astype(jnp.bfloat16) for c in range(CHUNKS)]
    last[0] = theirs[-1]
    back = [to_label(t, 1) for t in theirs]

    relayed, moved, low, high = {}, [], [], []
    for k in range(n_dp - 1, 0, -1):
        step = k & -k
        whole = g_own[k] * scale
        if step == k and k not in relayed:
            moved.append(to_dp(whole.astype(jnp.bfloat16), k))
            continue
        part = whole[direct:]
        for term in relayed.get(k, ()):
            part = part + term.astype(jnp.float32)
        part = part.astype(jnp.bfloat16)
        last[0] = part
        if step == k:
            high.append(to_dp(part, k))
        else:
            relayed.setdefault(k ^ step, []).append(in_turn(to_dp(part, step)))
        low.append(to_dp(whole[:direct].astype(jnp.bfloat16), k))
    grad_x = grad_x_of([d_own[k] for k in range(n_dp)])
    last[0] = grad_x
    grad_w = g_own[0] * scale
    for term in moved:
        grad_w = grad_w + in_turn(term).astype(jnp.float32)
    if high:
        rest, grad_w = grad_w[:direct], grad_w[direct:]
        for term in low:
            rest = rest + in_turn(term).astype(jnp.float32)
        for term in high:
            grad_w = grad_w + in_turn(term).astype(jnp.float32)
        grad_w = jnp.concatenate([rest, grad_w], axis=0)
    grad_w = grad_w.astype(jnp.bfloat16)
    last[0] = grad_w
    grad_x = (grad_x + jnp.concatenate([in_turn(b) for b in back], axis=0).astype(jnp.float32)).astype(jnp.bfloat16)
    return (grad_w, grad_x)


def solution(mesh):
    return jax.shard_map(
        local,
        mesh=mesh,
        in_specs=(
            P(("groups", "label", "dp"), None),
            P(("label", "dp"), None),
            P(("groups", "label", "dp"), None),
            P(("groups", "label", "dp")),
        ),
        out_specs=(P(("groups", "label", "dp"), None), P(("groups", "label", "dp"), None)),
        check_vma=False,
    )
```

```python
import math

import jax
import jax.numpy as jnp
from jax import lax
from jax.sharding import PartitionSpec as P

FIRST_RUN_THIRDS = 2
DIRECT_EIGHTHS = 2


def local(embeds, weights, pos_ids, pos_count):
    n_label = lax.axis_size("label")
    n_dp = lax.axis_size("dp")
    me_label = lax.axis_index("label")
    me_dp = lax.axis_index("dp")
    rows_dev, width = embeds.shape
    ch_dev = weights.shape[0]
    stretch = ch_dev * n_dp
    slots = pos_ids.shape[1]
    span = stretch * n_label // slots
    scale = 1.0 / math.sqrt(rows_dev * n_dp)
    cut = rows_dev * FIRST_RUN_THIRDS // 3
    runs = [slice(0, cut), slice(cut, rows_dev)]
    direct = ch_dev * DIRECT_EIGHTHS // 8
    valid = jnp.arange(slots, dtype=jnp.int32)[None, :] < pos_count[:, None]
    ids = jnp.where(valid, pos_ids, -1)
    last = [embeds]

    def in_turn(x):
        x, _ = lax.optimization_barrier((x, last[0]))
        return x

    def to_dp(x, k):
        return lax.ppermute(x, "dp", [(i, i ^ k) for i in range(n_dp)])

    def to_label(x, by):
        return lax.ppermute(x, "label", [(i, (i + by) % n_label) for i in range(n_label)])

    def delta_of(rows, row_ids, piece, k):
        start = me_label * stretch + (me_dp ^ k) * ch_dev
        column = lax.dynamic_slice_in_dim(row_ids, start // span, 1, axis=1)
        labels = start + jnp.arange(ch_dev, dtype=jnp.int32)
        target = (column == labels[None, :]).astype(jnp.float32)
        logits = lax.dot_general(
            rows, piece, (((1,), (1,)), ((), ())), preferred_element_type=jnp.float32
        )
        return (jax.nn.sigmoid(logits) - target).astype(jnp.bfloat16)

    def grad_w_of(delta, rows):
        return lax.dot_general(
            delta, rows, (((0,), (0,)), ((), ())), preferred_element_type=jnp.float32
        )

    def grad_x_of(deltas):
        return jnp.dot(
            in_turn(jnp.concatenate(deltas, axis=1)),
            jnp.concatenate([pieces[k] for k in range(n_dp)], axis=0),
            preferred_element_type=jnp.float32,
        )

    pieces = {0: weights}
    for k in range(1, n_dp):
        step = k & -k
        pieces[k] = to_dp(pieces[k ^ step], step)
    next_rows = [to_label(embeds[runs[0]], -1)]
    d_own, g_own = {}, {}
    d_next = [{} for _ in runs]

    def own_step(k):
        pieces[k] = in_turn(pieces[k])
        d_own[k] = delta_of(embeds, ids, pieces[k], k)
        g_own[k] = grad_w_of(d_own[k], embeds)
        last[0] = g_own[k]

    def next_step(c, k):
        d_next[c][k] = delta_of(next_rows[c], next_ids[runs[c]], in_turn(pieces[k]), k)
        g_own[k] = g_own[k] + grad_w_of(d_next[c][k], next_rows[c])
        last[0] = g_own[k]

    def send_back(c):
        theirs = grad_x_of([d_next[c][k] for k in range(n_dp)]).astype(jnp.bfloat16)
        last[0] = theirs
        return to_label(theirs, 1)

    next_ids = to_label(ids, -1)
    for k in [*range(1, min(2, n_dp)), 0, *range(2, n_dp - 1)]:
        own_step(k)
        if len(next_rows) < len(runs):
            next_rows.append(to_label(in_turn(embeds)[runs[1]], -1))
    next_ids = in_turn(next_ids)
    for k in range(n_dp - 2, -1, -1):
        next_step(0, k)
    if n_dp > 1:
        own_step(n_dp - 1)
        next_step(0, n_dp - 1)
    back = [send_back(0)]
    for k in range(n_dp - 1, -1, -1):
        next_step(1, k)
    back.append(send_back(1))

    relayed, moved, low, high = {}, [], [], []
    for k in range(n_dp - 1, 0, -1):
        step = k & -k
        whole = g_own[k] * scale
        if step == k and k not in relayed:
            moved.append(to_dp(whole.astype(jnp.bfloat16), k))
            continue
        part = whole[direct:]
        for term in relayed.get(k, ()):
            part = part + term.astype(jnp.float32)
        part = part.astype(jnp.bfloat16)
        last[0] = part
        if step == k:
            high.append(to_dp(part, k))
        else:
            relayed.setdefault(k ^ step, []).append(in_turn(to_dp(part, step)))
        low.append(to_dp(whole[:direct].astype(jnp.bfloat16), k))
    grad_x = grad_x_of([d_own[k] for k in range(n_dp)])
    last[0] = grad_x
    grad_w = g_own[0] * scale
    for term in moved:
        grad_w = grad_w + in_turn(term).astype(jnp.float32)
    if high:
        rest, grad_w = grad_w[:direct], grad_w[direct:]
        for term in low:
            rest = rest + in_turn(term).astype(jnp.float32)
        last[0] = rest
    first = jnp.pad(in_turn(back[0]), ((0, rows_dev - cut), (0, 0)))
    out_x = (grad_x + first.astype(jnp.float32)).astype(jnp.bfloat16)
    last[0] = out_x
    if high:
        for term in high:
            grad_w = grad_w + in_turn(term).astype(jnp.float32)
        grad_w = jnp.concatenate([rest, grad_w], axis=0)
    grad_w = grad_w.astype(jnp.bfloat16)
    last[0] = grad_w
    second = (grad_x[cut:] + in_turn(back[1]).astype(jnp.float32)).astype(jnp.bfloat16)
    grad_x = lax.dynamic_update_slice_in_dim(out_x, second, cut, axis=0)
    return (grad_w, grad_x)


def solution(mesh):
    return jax.shard_map(
        local,
        mesh=mesh,
        in_specs=(
            P(("groups", "label", "dp"), None),
            P(("label", "dp"), None),
            P(("groups", "label", "dp"), None),
            P(("groups", "label", "dp")),
        ),
        out_specs=(P(("groups", "label", "dp"), None), P(("groups", "label", "dp"), None)),
        check_vma=False,
    )
```

```python
import math

import jax
import jax.numpy as jnp
from jax import lax
from jax.sharding import PartitionSpec as P


def local(embeds, weights, pos_ids, pos_count):
    n_label = lax.axis_size("label")
    n_dp = lax.axis_size("dp")
    me_label = lax.axis_index("label")
    me_dp = lax.axis_index("dp")
    rows_dev, width = embeds.shape
    ch_dev = weights.shape[0]
    stretch = ch_dev * n_dp
    slots = pos_ids.shape[1]
    span = stretch * n_label // slots
    scale = 1.0 / math.sqrt(rows_dev * n_dp)
    valid = jnp.arange(slots, dtype=jnp.int32)[None, :] < pos_count[:, None]
    ids = jnp.where(valid, pos_ids, -1)
    last = [embeds]

    def in_turn(x):
        x, _ = lax.optimization_barrier((x, last[0]))
        return x

    def to_dp(x, k):
        return lax.ppermute(x, "dp", [(i, i ^ k) for i in range(n_dp)])

    def to_label(x, by):
        return lax.ppermute(x, "label", [(i, (i + by) % n_label) for i in range(n_label)])

    def delta_of(rows, row_ids, piece, k):
        start = me_label * stretch + (me_dp ^ k) * ch_dev
        column = lax.dynamic_slice_in_dim(row_ids, start // span, 1, axis=1)
        labels = start + jnp.arange(ch_dev, dtype=jnp.int32)
        target = (column == labels[None, :]).astype(jnp.float32)
        logits = lax.dot_general(
            rows, piece, (((1,), (1,)), ((), ())), preferred_element_type=jnp.float32
        )
        return (jax.nn.sigmoid(logits) - target).astype(jnp.bfloat16)

    def grad_w_of(delta, rows):
        return lax.dot_general(
            delta, rows, (((0,), (0,)), ((), ())), preferred_element_type=jnp.float32
        )

    def grad_x_of(deltas):
        return jnp.dot(
            in_turn(jnp.concatenate([deltas[k] for k in range(n_dp)], axis=1)),
            jnp.concatenate([pieces[k] for k in range(n_dp)], axis=0),
            preferred_element_type=jnp.float32,
        )

    pieces = {0: weights}
    for k in range(1, n_dp):
        step = k & -k
        pieces[k] = to_dp(pieces[k ^ step], step)
    next_rows = to_label(embeds, -1)
    d_own, d_next, g_w = {}, {}, {}

    def own_step(k):
        pieces[k] = in_turn(pieces[k])
        d_own[k] = delta_of(embeds, ids, pieces[k], k)
        g_w[k] = grad_w_of(d_own[k], embeds)
        last[0] = g_w[k]

    def next_step(k):
        d_next[k] = delta_of(next_rows, next_ids, in_turn(pieces[k]), k)
        last[0] = d_next[k]
        if k > 1:
            add_next(k)

    def add_next(k):
        g_w[k] = (g_w[k] + grad_w_of(in_turn(d_next[k]), next_rows)) * scale
        last[0] = g_w[k]

    own_step(1)
    next_ids = to_label(in_turn(ids), -1)
    for k in range(2, n_dp):
        own_step(k)
    next_ids = in_turn(next_ids)
    for k in range(n_dp - 1, -1, -1):
        next_step(k)
    theirs = grad_x_of(d_next).astype(jnp.bfloat16)
    last[0] = theirs
    back = to_label(theirs, 1)

    add_next(1)
    relayed, moved = {}, []
    for k in range(n_dp - 1, 0, -1):
        step = k & -k
        for term in relayed.get(k, ()):
            g_w[k] = g_w[k] + term.astype(jnp.float32)
        part = g_w[k].astype(jnp.bfloat16)
        if k in relayed:
            last[0] = part
        if step == k:
            moved.append(to_dp(part, k))
        else:
            relayed.setdefault(k ^ step, []).append(in_turn(to_dp(part, step)))
    own_step(0)
    grad_x = grad_x_of(d_own)
    last[0] = grad_x
    add_next(0)
    grad_w = g_w[0]
    for term in reversed(moved):
        grad_w = grad_w + in_turn(term).astype(jnp.float32)
    grad_w = grad_w.astype(jnp.bfloat16)
    last[0] = grad_w
    grad_x = (grad_x + in_turn(back).astype(jnp.float32)).astype(jnp.bfloat16)
    return (grad_w, grad_x)


def solution(mesh):
    return jax.shard_map(
        local,
        mesh=mesh,
        in_specs=(
            P(("groups", "label", "dp"), None),
            P(("label", "dp"), None),
            P(("groups", "label", "dp"), None),
            P(("groups", "label", "dp")),
        ),
        out_specs=(P(("groups", "label", "dp"), None), P(("groups", "label", "dp"), None)),
        check_vma=False,
    )
```

```python
import math

import jax
import jax.numpy as jnp
from jax import lax
from jax.sharding import PartitionSpec as P


DIRECT_EIGHTHS = 2


def local(embeds, weights, pos_ids, pos_count):
    n_label = lax.axis_size("label")
    n_dp = lax.axis_size("dp")
    me_label = lax.axis_index("label")
    me_dp = lax.axis_index("dp")
    rows_dev, width = embeds.shape
    ch_dev = weights.shape[0]
    stretch = ch_dev * n_dp
    slots = pos_ids.shape[1]
    span = stretch * n_label // slots
    scale = 1.0 / math.sqrt(rows_dev * n_dp)
    valid = jnp.arange(slots, dtype=jnp.int32)[None, :] < pos_count[:, None]
    ids = jnp.where(valid, pos_ids, -1)
    direct = ch_dev * DIRECT_EIGHTHS // 8
    last = [embeds]

    def in_turn(x):
        x, _ = lax.optimization_barrier((x, last[0]))
        return x

    def to_dp(x, k):
        return lax.ppermute(x, "dp", [(i, i ^ k) for i in range(n_dp)])

    def to_label(x, by):
        return lax.ppermute(x, "label", [(i, (i + by) % n_label) for i in range(n_label)])

    def delta_of(rows, row_ids, piece, ks):
        starts = [me_label * stretch + (me_dp ^ k) * ch_dev for k in ks]
        place = jnp.arange(len(ks) * ch_dev, dtype=jnp.int32)[None, :]
        for i, start in enumerate(starts):
            column = lax.dynamic_slice_in_dim(row_ids, start // span, 1, axis=1) - (start - i * ch_dev)
            sought = column if i == 0 else jnp.where(place < i * ch_dev, sought, column)
        target = (sought == place).astype(jnp.float32)
        logits = lax.dot_general(
            rows, piece, (((1,), (1,)), ((), ())), preferred_element_type=jnp.float32
        )
        return (jax.nn.sigmoid(logits) - target).astype(jnp.bfloat16)

    def grad_w_of(delta, rows):
        return lax.dot_general(
            delta, rows, (((0,), (0,)), ((), ())), preferred_element_type=jnp.float32
        )

    def grad_x_of(deltas):
        return jnp.dot(
            in_turn(jnp.concatenate(deltas, axis=1)),
            jnp.concatenate([pieces[k] for k in range(n_dp)], axis=0),
            preferred_element_type=jnp.float32,
        )

    pieces = {0: weights}
    for k in range(1, n_dp):
        step = k & -k
        pieces[k] = to_dp(pieces[k ^ step], step)
    next_rows = to_label(embeds, -1)
    d_own, g_own, g_w = {}, {}, {}

    def own_step(k):
        pieces[k] = in_turn(pieces[k])
        d_own[k] = delta_of(embeds, ids, pieces[k], [k])
        g_own[k] = grad_w_of(d_own[k], embeds)
        last[0] = g_own[k]

    def add_next(k):
        g_w[k] = (g_own[k] + grad_w_of(in_turn(d_next[:, k * ch_dev:(k + 1) * ch_dev]), next_rows)) * scale
        last[0] = g_w[k]

    early, late = list(range(n_dp - 1)), n_dp - 1
    own_step(0)
    next_ids = to_label(in_turn(ids), -1)
    own_step(1)
    next_rows, next_ids, _ = lax.optimization_barrier((next_rows, next_ids, last[0]))
    d_early = delta_of(
        in_turn(next_rows), next_ids, jnp.concatenate([pieces[k] for k in early], axis=0), early
    )
    last[0] = d_early
    d_late = delta_of(next_rows, next_ids, in_turn(pieces[late]), [late])
    d_next = jnp.concatenate([d_early, d_late], axis=1)
    last[0] = d_next
    theirs = grad_x_of([d_next]).astype(jnp.bfloat16)
    last[0] = theirs
    back = to_label(theirs, 1)

    relayed, moved, low, high = {}, [], [], []
    for k in [k for k in range(late, 0, -1) if k not in g_own] + [1]:
        if k not in g_own:
            own_step(k)
        add_next(k)
    for k in range(late, 0, -1):
        step = k & -k
        whole = g_w[k]
        if step == k and k not in relayed:
            moved.append(to_dp(whole.astype(jnp.bfloat16), k))
            continue
        part = whole[direct:]
        for term in relayed.get(k, ()):
            part = part + term.astype(jnp.float32)
        part = part.astype(jnp.bfloat16)
        last[0] = part
        if step == k:
            high.append(to_dp(part, k))
        else:
            relayed.setdefault(k ^ step, []).append(in_turn(to_dp(part, step)))
        if direct:
            low.append(to_dp(in_turn(whole)[:direct].astype(jnp.bfloat16), k))
    grad_x = grad_x_of([d_own[k] for k in range(n_dp)])
    last[0] = grad_x
    add_next(0)
    grad_w = g_w[0]
    for term in moved:
        grad_w = grad_w + in_turn(term).astype(jnp.float32)
    if high:
        rest, grad_w = grad_w[:direct], grad_w[direct:]
        for term in low:
            rest = rest + in_turn(term).astype(jnp.float32)
        for term in high:
            grad_w = grad_w + in_turn(term).astype(jnp.float32)
        grad_w = jnp.concatenate([rest, grad_w], axis=0)
    grad_w = grad_w.astype(jnp.bfloat16)
    last[0] = grad_w
    grad_x = (grad_x + in_turn(back).astype(jnp.float32)).astype(jnp.bfloat16)
    return (grad_w, grad_x)


def solution(mesh):
    return jax.shard_map(
        local,
        mesh=mesh,
        in_specs=(
            P(("groups", "label", "dp"), None),
            P(("label", "dp"), None),
            P(("groups", "label", "dp"), None),
            P(("groups", "label", "dp")),
        ),
        out_specs=(P(("groups", "label", "dp"), None), P(("groups", "label", "dp"), None)),
        check_vma=False,
    )
```

```python
import math

import jax
import jax.numpy as jnp
from jax import lax
from jax.sharding import PartitionSpec as P


SCATTER_DIRECT_EIGHTHS = 2
GATHER_DIRECT_EIGHTHS = 4


def local(embeds, weights, pos_ids, pos_count):
    n_label = lax.axis_size("label")
    n_dp = lax.axis_size("dp")
    me_label = lax.axis_index("label")
    me_dp = lax.axis_index("dp")
    rows_dev, width = embeds.shape
    ch_dev = weights.shape[0]
    stretch = ch_dev * n_dp
    slots = pos_ids.shape[1]
    span = stretch * n_label // slots
    scale = 1.0 / math.sqrt(rows_dev * n_dp)
    valid = jnp.arange(slots, dtype=jnp.int32)[None, :] < pos_count[:, None]
    ids = jnp.where(valid, pos_ids, -1)
    direct = ch_dev * SCATTER_DIRECT_EIGHTHS // 8
    ahead = ch_dev * GATHER_DIRECT_EIGHTHS // 8
    last = [embeds]

    def in_turn(x):
        x, _ = lax.optimization_barrier((x, last[0]))
        return x

    def to_dp(x, k):
        return lax.ppermute(x, "dp", [(i, i ^ k) for i in range(n_dp)])

    def to_label(x, by):
        return lax.ppermute(x, "label", [(i, (i + by) % n_label) for i in range(n_label)])

    def delta_of(rows, row_ids, piece, k):
        start = me_label * stretch + (me_dp ^ k) * ch_dev
        column = lax.dynamic_slice_in_dim(row_ids, start // span, 1, axis=1)
        labels = start + jnp.arange(ch_dev, dtype=jnp.int32)
        target = (column == labels[None, :]).astype(jnp.float32)
        logits = lax.dot_general(
            rows, piece, (((1,), (1,)), ((), ())), preferred_element_type=jnp.float32
        )
        return (jax.nn.sigmoid(logits) - target).astype(jnp.bfloat16)

    def grad_w_of(delta, rows):
        return lax.dot_general(
            delta, rows, (((0,), (0,)), ((), ())), preferred_element_type=jnp.float32
        )

    def grad_x_of(deltas):
        return jnp.dot(
            in_turn(jnp.concatenate([deltas[k] for k in range(n_dp)], axis=1)),
            jnp.concatenate([pieces[k] for k in range(n_dp)], axis=0),
            preferred_element_type=jnp.float32,
        )

    pieces = {0: weights}
    for k in range(2, n_dp):
        if k & -k == k:
            pieces[k] = to_dp(weights, k)
    next_rows = to_label(embeds, -1)
    d_own, g_own, g_w = {}, {}, {}

    def own_step(k):
        pieces[k] = in_turn(pieces[k])
        d_own[k] = delta_of(embeds, ids, pieces[k], k)
        g_own[k] = grad_w_of(d_own[k], embeds)
        last[0] = g_own[k]

    def add_next(k):
        g_w[k] = (g_own[k] + grad_w_of(in_turn(d_next[k]), next_rows)) * scale
        last[0] = g_w[k]

    late = n_dp - 1
    own_step(0)
    later = in_turn(weights)
    pieces[1] = to_dp(later, 1)
    for k in range(2, n_dp):
        step = k & -k
        if step < k:
            pieces[k] = jnp.concatenate(
                [to_dp(later[:ahead], k), to_dp(pieces[k ^ step][ahead:], step)], axis=0
            )
    next_ids = to_label(in_turn(ids), -1)
    for k in range(1, n_dp):
        own_step(k)
    next_rows, next_ids, _ = lax.optimization_barrier((next_rows, next_ids, last[0]))
    d_next = {}
    for k in range(late, -1, -1):
        d_next[k] = delta_of(next_rows, next_ids, in_turn(pieces[k]), k)
        last[0] = d_next[k]
    theirs = grad_x_of(d_next).astype(jnp.bfloat16)
    last[0] = theirs
    back = to_label(theirs, 1)

    relayed, moved, low, high = {}, [], [], []
    for k in range(late, 0, -1):
        add_next(k)
    for k in range(late, 0, -1):
        step = k & -k
        whole = g_w[k]
        if step == k and k not in relayed:
            moved.append(to_dp(whole.astype(jnp.bfloat16), k))
            continue
        part = whole[direct:]
        for term in relayed.get(k, ()):
            part = part + term.astype(jnp.float32)
        part = part.astype(jnp.bfloat16)
        last[0] = part
        if step == k:
            high.append(to_dp(part, k))
        else:
            relayed.setdefault(k ^ step, []).append(in_turn(to_dp(part, step)))
        if direct:
            low.append(to_dp(in_turn(whole)[:direct].astype(jnp.bfloat16), k))
    grad_x = grad_x_of(d_own)
    last[0] = grad_x
    add_next(0)
    grad_w = g_w[0]
    for term in moved:
        grad_w = grad_w + in_turn(term).astype(jnp.float32)
    if high:
        rest, grad_w = grad_w[:direct], grad_w[direct:]
        for term in low:
            rest = rest + in_turn(term).astype(jnp.float32)
        for term in high:
            grad_w = grad_w + in_turn(term).astype(jnp.float32)
        grad_w = jnp.concatenate([rest, grad_w], axis=0)
    grad_w = grad_w.astype(jnp.bfloat16)
    last[0] = grad_w
    grad_x = (grad_x + in_turn(back).astype(jnp.float32)).astype(jnp.bfloat16)
    return (grad_w, grad_x)


def solution(mesh):
    return jax.shard_map(
        local,
        mesh=mesh,
        in_specs=(
            P(("groups", "label", "dp"), None),
            P(("label", "dp"), None),
            P(("groups", "label", "dp"), None),
            P(("groups", "label", "dp")),
        ),
        out_specs=(P(("groups", "label", "dp"), None), P(("groups", "label", "dp"), None)),
        check_vma=False,
    )
```

```python
import math

import jax
import jax.numpy as jnp
from jax import lax
from jax.sharding import PartitionSpec as P


SCATTER_DIRECT_EIGHTHS = 2
GATHER_DIRECT_EIGHTHS = 4


def local(embeds, weights, pos_ids, pos_count):
    n_groups = lax.axis_size("groups")
    n_label = lax.axis_size("label")
    n_dp = lax.axis_size("dp")
    me_group = lax.axis_index("groups")
    me_label = lax.axis_index("label")
    me_dp = lax.axis_index("dp")
    rows_dev, width = embeds.shape
    ch_dev = weights.shape[0]
    stretch = ch_dev * n_dp
    slots = pos_ids.shape[1]
    span = stretch * n_label // slots
    scale = 1.0 / math.sqrt(rows_dev * n_dp)
    valid = jnp.arange(slots, dtype=jnp.int32)[None, :] < pos_count[:, None]
    ids = jnp.where(valid, pos_ids, -1)
    direct = ch_dev * SCATTER_DIRECT_EIGHTHS // 8
    ahead = ch_dev * GATHER_DIRECT_EIGHTHS // 8
    last = [embeds]

    def in_turn(x):
        x, _ = lax.optimization_barrier((x, last[0]))
        return x

    def to_dp(x, k):
        return lax.ppermute(x, "dp", [(i, i ^ k) for i in range(n_dp)])

    def to_label(x, by):
        return lax.ppermute(x, "label", [(i, (i + by) % n_label) for i in range(n_label)])

    def delta_of(rows, row_ids, piece, k):
        start = me_label * stretch + (me_dp ^ k) * ch_dev
        column = lax.dynamic_slice_in_dim(row_ids, start // span, 1, axis=1)
        labels = start + jnp.arange(ch_dev, dtype=jnp.int32)
        target = (column == labels[None, :]).astype(jnp.float32)
        logits = lax.dot_general(
            rows, piece, (((1,), (1,)), ((), ())), preferred_element_type=jnp.float32
        )
        return (jax.nn.sigmoid(logits) - target).astype(jnp.bfloat16)

    def grad_w_of(delta, rows):
        return lax.dot_general(
            delta, rows, (((0,), (0,)), ((), ())), preferred_element_type=jnp.float32
        )

    def grad_x_of(deltas):
        return jnp.dot(
            in_turn(jnp.concatenate([deltas[k] for k in range(n_dp)], axis=1)),
            jnp.concatenate([pieces[k] for k in range(n_dp)], axis=0),
            preferred_element_type=jnp.float32,
        )

    pieces = {0: weights}
    for k in range(2, n_dp):
        if k & -k == k:
            pieces[k] = to_dp(weights, k)
    half = ch_dev // 2
    after_ids, _ = lax.optimization_barrier((weights, ids))
    near = to_dp(jnp.where(me_group == 0, after_ids[:half], after_ids[half:]), 1)
    next_rows = to_label(embeds, -1)
    d_own, g_own, g_w = {}, {}, {}

    def own_step(k):
        pieces[k] = in_turn(pieces[k])
        d_own[k] = delta_of(embeds, ids, pieces[k], k)
        g_own[k] = grad_w_of(d_own[k], embeds)
        last[0] = g_own[k]

    def add_next(k):
        g_w[k] = (g_own[k] + grad_w_of(in_turn(d_next[k]), next_rows)) * scale
        last[0] = g_w[k]

    late = n_dp - 1
    own_step(0)
    later = in_turn(weights)
    near = in_turn(near)
    other = lax.ppermute(near, "groups", [(i, i ^ 1) for i in range(n_groups)])
    pieces[1] = jnp.where(
        me_group == 0, jnp.concatenate([near, other], axis=0), jnp.concatenate([other, near], axis=0)
    )
    for k in range(2, n_dp):
        step = k & -k
        if step < k:
            pieces[k] = jnp.concatenate(
                [to_dp(later[:ahead], k), to_dp(pieces[k ^ step][ahead:], step)], axis=0
            )
    next_ids = to_label(in_turn(ids), -1)
    for k in range(1, n_dp):
        own_step(k)
    next_rows, next_ids, _ = lax.optimization_barrier((next_rows, next_ids, last[0]))
    d_next = {}
    for k in range(late, -1, -1):
        d_next[k] = delta_of(next_rows, next_ids, in_turn(pieces[k]), k)
        last[0] = d_next[k]
    theirs = grad_x_of(d_next).astype(jnp.bfloat16)
    last[0] = theirs
    back = to_label(theirs, 1)

    relayed, moved, low, high = {}, [], [], []
    for k in range(late, 0, -1):
        add_next(k)
    for k in range(late, 0, -1):
        step = k & -k
        whole = g_w[k]
        if step == k and k not in relayed:
            moved.append(to_dp(whole.astype(jnp.bfloat16), k))
            continue
        part = whole[direct:]
        for term in relayed.get(k, ()):
            part = part + term.astype(jnp.float32)
        part = part.astype(jnp.bfloat16)
        last[0] = part
        if step == k:
            high.append(to_dp(part, k))
        else:
            relayed.setdefault(k ^ step, []).append(in_turn(to_dp(part, step)))
        if direct:
            low.append(to_dp(in_turn(whole)[:direct].astype(jnp.bfloat16), k))
    grad_x = grad_x_of(d_own)
    last[0] = grad_x
    add_next(0)
    grad_w = g_w[0]
    for term in moved:
        grad_w = grad_w + in_turn(term).astype(jnp.float32)
    if high:
        rest, grad_w = grad_w[:direct], grad_w[direct:]
        for term in low:
            rest = rest + in_turn(term).astype(jnp.float32)
        for term in high:
            grad_w = grad_w + in_turn(term).astype(jnp.float32)
        grad_w = jnp.concatenate([rest, grad_w], axis=0)
    grad_w = grad_w.astype(jnp.bfloat16)
    last[0] = grad_w
    grad_x = (grad_x + in_turn(back).astype(jnp.float32)).astype(jnp.bfloat16)
    return (grad_w, grad_x)


def solution(mesh):
    return jax.shard_map(
        local,
        mesh=mesh,
        in_specs=(
            P(("groups", "label", "dp"), None),
            P(("label", "dp"), None),
            P(("groups", "label", "dp"), None),
            P(("groups", "label", "dp")),
        ),
        out_specs=(P(("groups", "label", "dp"), None), P(("groups", "label", "dp"), None)),
        check_vma=False,
    )
```

```python
import math

import jax
import jax.numpy as jnp
from jax import lax
from jax.sharding import PartitionSpec as P


SCATTER_DIRECT_EIGHTHS = 2


def local(embeds, weights, pos_ids, pos_count):
    n_label = lax.axis_size("label")
    n_dp = lax.axis_size("dp")
    me_label = lax.axis_index("label")
    me_dp = lax.axis_index("dp")
    rows_dev, width = embeds.shape
    ch_dev = weights.shape[0]
    stretch = ch_dev * n_dp
    slots = pos_ids.shape[1]
    span = stretch * n_label // slots
    scale = 1.0 / math.sqrt(rows_dev * n_dp)
    valid = jnp.arange(slots, dtype=jnp.int32)[None, :] < pos_count[:, None]
    ids = jnp.where(valid, pos_ids, -1)
    direct = ch_dev * SCATTER_DIRECT_EIGHTHS // 8
    last = [embeds]

    def in_turn(x):
        x, _ = lax.optimization_barrier((x, last[0]))
        return x

    def to_dp(x, k):
        return lax.ppermute(x, "dp", [(i, i ^ k) for i in range(n_dp)])

    def to_label(x, by):
        return lax.ppermute(x, "label", [(i, (i + by) % n_label) for i in range(n_label)])

    def delta_of(rows, row_ids, piece, k):
        start = me_label * stretch + (me_dp ^ k) * ch_dev
        column = lax.dynamic_slice_in_dim(row_ids, start // span, 1, axis=1)
        labels = start + jnp.arange(ch_dev, dtype=jnp.int32)
        target = (column == labels[None, :]).astype(jnp.float32)
        logits = lax.dot_general(
            rows, piece, (((1,), (1,)), ((), ())), preferred_element_type=jnp.float32
        )
        return (jax.nn.sigmoid(logits) - target).astype(jnp.bfloat16)

    def grad_w_of(delta, rows):
        return lax.dot_general(
            delta, rows, (((0,), (0,)), ((), ())), preferred_element_type=jnp.float32
        )

    def grad_x_of(deltas):
        return jnp.dot(
            in_turn(jnp.concatenate([deltas[k] for k in range(n_dp)], axis=1)),
            jnp.concatenate([pieces[k] for k in range(n_dp)], axis=0),
            preferred_element_type=jnp.float32,
        )

    late = n_dp - 1
    pieces = {0: weights}
    for k in range(2, n_dp):
        step = k & -k
        pieces[k] = to_dp(pieces[k ^ step], step)
    next_rows = to_label(embeds, -1)
    d_own, g_own, g_w = {}, {}, {}

    def own_step(k):
        pieces[k] = in_turn(pieces[k])
        d_own[k] = delta_of(embeds, ids, pieces[k], k)
        last[0] = d_own[k]
        if k == 0:
            pieces[1] = to_dp(in_turn(weights), 1)
        g_own[k] = grad_w_of(d_own[k], embeds)
        last[0] = g_own[k]

    def add_next(k):
        g_w[k] = (g_own[k] + grad_w_of(in_turn(d_next[k]), next_rows)) * scale
        last[0] = g_w[k]

    late = n_dp - 1
    def next_delta(k):
        d_next[k] = delta_of(next_rows, next_ids, in_turn(pieces[k]), k)
        last[0] = d_next[k]

    d_next = {}
    own_step(0)
    next_ids = to_label(in_turn(ids), -1)
    own_step(1)
    next_rows, next_ids, _ = lax.optimization_barrier((next_rows, next_ids, last[0]))
    for k in range(late):
        next_delta(k)
    for k in range(2, late):
        own_step(k)
    next_delta(late)
    own_step(late)
    add_next(late)
    theirs = grad_x_of(d_next).astype(jnp.bfloat16)
    last[0] = theirs
    back = to_label(theirs, 1)

    relayed, moved, low, high = {}, [], [], []
    for k in range(late - 1, 1, -1):
        add_next(k)
    for k in range(late, 1, -1):
        low.append(to_dp(in_turn(g_w[k])[:direct].astype(jnp.bfloat16), k))
    for k in range(late, 0, -1):
        step = k & -k
        if k == 1:
            add_next(k)
            moved.append(to_dp(g_w[k].astype(jnp.bfloat16), k))
            continue
        part = g_w[k][direct:]
        for term in relayed.get(k, ()):
            part = part + term.astype(jnp.float32)
        part = part.astype(jnp.bfloat16)
        if k in relayed:
            last[0] = part
        if step == k:
            high.append(to_dp(part, k))
        else:
            relayed.setdefault(k ^ step, []).append(in_turn(to_dp(part, step)))
    grad_x = grad_x_of(d_own)
    last[0] = grad_x
    add_next(0)
    grad_w = g_w[0]
    for term in moved:
        grad_w = grad_w + in_turn(term).astype(jnp.float32)
    rest, grad_w = grad_w[:direct], grad_w[direct:]
    for term in low:
        rest = rest + in_turn(term).astype(jnp.float32)
    for term in high:
        grad_w = grad_w + in_turn(term).astype(jnp.float32)
    grad_w = jnp.concatenate([rest, grad_w], axis=0).astype(jnp.bfloat16)
    last[0] = grad_w
    grad_x = (grad_x + in_turn(back).astype(jnp.float32)).astype(jnp.bfloat16)
    return (grad_w, grad_x)


def solution(mesh):
    return jax.shard_map(
        local,
        mesh=mesh,
        in_specs=(
            P(("groups", "label", "dp"), None),
            P(("label", "dp"), None),
            P(("groups", "label", "dp"), None),
            P(("groups", "label", "dp")),
        ),
        out_specs=(P(("groups", "label", "dp"), None), P(("groups", "label", "dp"), None)),
        check_vma=False,
    )
```

```python
import math

import jax
import jax.numpy as jnp
from jax import lax
from jax.sharding import PartitionSpec as P


def local(embeds, weights, pos_ids, pos_count):
    n_label = lax.axis_size("label")
    n_dp = lax.axis_size("dp")
    me_label = lax.axis_index("label")
    me_dp = lax.axis_index("dp")
    rows_dev, width = embeds.shape
    ch_dev = weights.shape[0]
    stretch = ch_dev * n_dp
    slots = pos_ids.shape[1]
    span = stretch * n_label // slots
    scale = 1.0 / math.sqrt(rows_dev * n_dp)
    valid = jnp.arange(slots, dtype=jnp.int32)[None, :] < pos_count[:, None]
    ids = jnp.where(valid, pos_ids, -1)
    last = [embeds]

    def in_turn(x):
        x, _ = lax.optimization_barrier((x, last[0]))
        return x

    def to_dp(x, k):
        return lax.ppermute(x, "dp", [(i, i ^ k) for i in range(n_dp)])

    def to_label(x, by):
        return lax.ppermute(x, "label", [(i, (i + by) % n_label) for i in range(n_label)])

    def delta_of(rows, row_ids, piece, ks):
        starts = [me_label * stretch + (me_dp ^ k) * ch_dev for k in ks]
        place = jnp.arange(len(ks) * ch_dev, dtype=jnp.int32)[None, :]
        for i, start in enumerate(starts):
            column = lax.dynamic_slice_in_dim(row_ids, start // span, 1, axis=1) - (start - i * ch_dev)
            sought = column if i == 0 else jnp.where(place < i * ch_dev, sought, column)
        target = (sought == place).astype(jnp.float32)
        logits = lax.dot_general(
            rows, piece, (((1,), (1,)), ((), ())), preferred_element_type=jnp.float32
        )
        return (jax.nn.sigmoid(logits) - target).astype(jnp.bfloat16)

    def grad_w_of(delta, rows):
        return lax.dot_general(
            delta, rows, (((0,), (0,)), ((), ())), preferred_element_type=jnp.float32
        )

    late = n_dp - 1
    pieces = {0: weights}
    for k in range(1, n_dp):
        step = k & -k
        pieces[k] = to_dp(pieces[k ^ step], step)
    next_rows = to_label(embeds, -1)
    d_own, g_w = {}, {}

    def own_step(k):
        pieces[k] = in_turn(pieces[k])
        d_own[k] = delta_of(embeds, ids, pieces[k], [k])
        g_w[k] = grad_w_of(d_own[k], embeds)
        last[0] = g_w[k]

    def add_next(k):
        delta = in_turn(d_next)[:, k * ch_dev:(k + 1) * ch_dev]
        g_w[k] = (g_w[k] + grad_w_of(delta, next_rows)) * scale
        last[0] = g_w[k]

    own_step(0)
    next_ids = to_label(in_turn(ids), -1)
    for k in range(1, n_dp):
        own_step(k)
    joined = in_turn(jnp.concatenate([pieces[k] for k in range(n_dp)], axis=0))
    joined = lax.optimization_barrier(joined)
    last[0] = joined
    next_ids = in_turn(next_ids)
    d_next = delta_of(next_rows, next_ids, joined, list(range(n_dp)))
    last[0] = d_next
    add_next(late)
    theirs = jnp.dot(in_turn(d_next), joined, preferred_element_type=jnp.float32).astype(jnp.bfloat16)
    last[0] = theirs
    back = to_label(theirs, 1)
    for k in range(late - 1, 0, -1):
        add_next(k)

    relayed, moved = {}, []
    for k in range(late, 0, -1):
        step = k & -k
        for term in relayed.get(k, ()):
            g_w[k] = g_w[k] + term.astype(jnp.float32)
        part = g_w[k].astype(jnp.bfloat16)
        if k in relayed:
            last[0] = part
        if step == k:
            moved.append(to_dp(part, k))
        else:
            relayed.setdefault(k ^ step, []).append(in_turn(to_dp(part, step)))
    grad_x = jnp.dot(
        in_turn(jnp.concatenate([d_own[k] for k in range(n_dp)], axis=1)),
        joined,
        preferred_element_type=jnp.float32,
    )
    last[0] = grad_x
    add_next(0)
    grad_w = g_w[0]
    for term in reversed(moved):
        grad_w = grad_w + in_turn(term).astype(jnp.float32)
    grad_w = grad_w.astype(jnp.bfloat16)
    last[0] = grad_w
    grad_x = (grad_x + in_turn(back).astype(jnp.float32)).astype(jnp.bfloat16)
    return (grad_w, grad_x)


def solution(mesh):
    return jax.shard_map(
        local,
        mesh=mesh,
        in_specs=(
            P(("groups", "label", "dp"), None),
            P(("label", "dp"), None),
            P(("groups", "label", "dp"), None),
            P(("groups", "label", "dp")),
        ),
        out_specs=(P(("groups", "label", "dp"), None), P(("groups", "label", "dp"), None)),
        check_vma=False,
    )
```

```python
import math

import jax
import jax.numpy as jnp
from jax import lax
from jax.sharding import PartitionSpec as P


def local(embeds, weights, pos_ids, pos_count):
    n_label = lax.axis_size("label")
    n_dp = lax.axis_size("dp")
    me_label = lax.axis_index("label")
    me_dp = lax.axis_index("dp")
    rows_dev, width = embeds.shape
    ch_dev = weights.shape[0]
    stretch = ch_dev * n_dp
    slots = pos_ids.shape[1]
    span = stretch * n_label // slots
    scale = 1.0 / math.sqrt(rows_dev * n_dp)
    valid = jnp.arange(slots, dtype=jnp.int32)[None, :] < pos_count[:, None]
    ids = jnp.where(valid, pos_ids, -1)
    last = [embeds]

    def in_turn(x):
        x, _ = lax.optimization_barrier((x, last[0]))
        return x

    def to_dp(x, k):
        return lax.ppermute(x, "dp", [(i, i ^ k) for i in range(n_dp)])

    def to_label(x, by):
        return lax.ppermute(x, "label", [(i, (i + by) % n_label) for i in range(n_label)])

    def delta_of(rows, row_ids, piece, ks):
        starts = [me_label * stretch + (me_dp ^ k) * ch_dev for k in ks]
        place = jnp.arange(len(ks) * ch_dev, dtype=jnp.int32)[None, :]
        for i, start in enumerate(starts):
            column = lax.dynamic_slice_in_dim(row_ids, start // span, 1, axis=1) - (start - i * ch_dev)
            sought = column if i == 0 else jnp.where(place < i * ch_dev, sought, column)
        target = (sought == place).astype(jnp.float32)
        logits = lax.dot_general(
            rows, piece, (((1,), (1,)), ((), ())), preferred_element_type=jnp.float32
        )
        return (jax.nn.sigmoid(logits) - target).astype(jnp.bfloat16)

    def grad_w_of(delta, rows):
        return lax.dot_general(
            delta, rows, (((0,), (0,)), ((), ())), preferred_element_type=jnp.float32
        )

    late = n_dp - 1
    pieces = {0: weights}
    for k in range(1, n_dp):
        step = k & -k
        pieces[k] = to_dp(pieces[k ^ step], step)
    next_rows = to_label(embeds, -1)
    d_own, g_w = {}, {}
    joined = [jnp.zeros((stretch, width), weights.dtype)]

    def own_step(k):
        pieces[k] = in_turn(pieces[k])
        d_own[k] = delta_of(embeds, ids, pieces[k], [k])
        g_w[k] = grad_w_of(d_own[k], embeds)
        joined[0] = lax.dynamic_update_slice_in_dim(joined[0], pieces[k], k * ch_dev, axis=0)
        last[0] = g_w[k]

    def add_next(k):
        delta = in_turn(d_next)[:, k * ch_dev:(k + 1) * ch_dev]
        g_w[k] = (g_w[k] + grad_w_of(delta, next_rows)) * scale
        last[0] = g_w[k]

    own_step(0)
    next_ids = to_label(in_turn(ids), -1)
    for k in range(1, n_dp):
        own_step(k)
    joined = joined[0]
    next_ids = in_turn(next_ids)
    d_next = delta_of(next_rows, next_ids, joined, list(range(n_dp)))
    last[0] = d_next
    add_next(late)
    theirs = jnp.dot(in_turn(d_next), joined, preferred_element_type=jnp.float32).astype(jnp.bfloat16)
    last[0] = theirs
    back = to_label(theirs, 1)
    for k in range(1, late):
        add_next(k)

    relayed, moved = {}, []
    for k in range(late, 0, -1):
        step = k & -k
        for term in relayed.get(k, ()):
            g_w[k] = g_w[k] + term.astype(jnp.float32)
        part = g_w[k].astype(jnp.bfloat16)
        if k in relayed:
            last[0] = part
        if step == k:
            moved.append(to_dp(part, k))
        else:
            relayed.setdefault(k ^ step, []).append(in_turn(to_dp(part, step)))
    grad_x = jnp.dot(
        in_turn(jnp.concatenate([d_own[k] for k in range(n_dp)], axis=1)),
        joined,
        preferred_element_type=jnp.float32,
    )
    last[0] = grad_x
    add_next(0)
    grad_w = g_w[0]
    for term in reversed(moved):
        grad_w = grad_w + in_turn(term).astype(jnp.float32)
    grad_w = grad_w.astype(jnp.bfloat16)
    last[0] = grad_w
    grad_x = (grad_x + in_turn(back).astype(jnp.float32)).astype(jnp.bfloat16)
    return (grad_w, grad_x)


def solution(mesh):
    return jax.shard_map(
        local,
        mesh=mesh,
        in_specs=(
            P(("groups", "label", "dp"), None),
            P(("label", "dp"), None),
            P(("groups", "label", "dp"), None),
            P(("groups", "label", "dp")),
        ),
        out_specs=(P(("groups", "label", "dp"), None), P(("groups", "label", "dp"), None)),
        check_vma=False,
    )
```

```python
import math

import jax
import jax.numpy as jnp
from jax import lax
from jax.sharding import PartitionSpec as P


def local(embeds, weights, pos_ids, pos_count):
    n_label = lax.axis_size("label")
    n_dp = lax.axis_size("dp")
    me_label = lax.axis_index("label")
    me_dp = lax.axis_index("dp")
    rows_dev, width = embeds.shape
    ch_dev = weights.shape[0]
    stretch = ch_dev * n_dp
    slots = pos_ids.shape[1]
    span = stretch * n_label // slots
    scale = 1.0 / math.sqrt(rows_dev * n_dp)
    valid = jnp.arange(slots, dtype=jnp.int32)[None, :] < pos_count[:, None]
    ids = jnp.where(valid, pos_ids, -1)
    last = [embeds]

    def in_turn(x):
        x, _ = lax.optimization_barrier((x, last[0]))
        return x

    def to_dp(x, k):
        return lax.ppermute(x, "dp", [(i, i ^ k) for i in range(n_dp)])

    def to_label(x, by):
        return lax.ppermute(x, "label", [(i, (i + by) % n_label) for i in range(n_label)])

    def delta_of(rows, row_ids, piece, ks):
        starts = [me_label * stretch + (me_dp ^ k) * ch_dev for k in ks]
        place = jnp.arange(len(ks) * ch_dev, dtype=jnp.int32)[None, :]
        for i, start in enumerate(starts):
            column = lax.dynamic_slice_in_dim(row_ids, start // span, 1, axis=1) - (start - i * ch_dev)
            sought = column if i == 0 else jnp.where(place < i * ch_dev, sought, column)
        target = (sought == place).astype(jnp.float32)
        logits = lax.dot_general(
            rows, piece, (((1,), (1,)), ((), ())), preferred_element_type=jnp.float32
        )
        return (jax.nn.sigmoid(logits) - target).astype(jnp.bfloat16)

    def grad_w_of(delta, rows):
        return lax.dot_general(
            delta, rows, (((0,), (0,)), ((), ())), preferred_element_type=jnp.float32
        )

    late = n_dp - 1
    pieces = {0: weights}
    for k in range(1, n_dp):
        step = k & -k
        pieces[k] = to_dp(pieces[k ^ step], step)
    d_own, g_w = {}, {}
    joined = [jnp.zeros((stretch, width), weights.dtype)]
    next_rows = to_label(embeds, -1)

    def join(piece, at):
        joined[0] = lax.dynamic_update_slice_in_dim(joined[0], piece, at, axis=0)

    def own_delta(k, piece):
        d_own[k] = delta_of(embeds, ids, in_turn(piece), [k])
        last[0] = d_own[k]

    def own_grad(k):
        g_w[k] = grad_w_of(in_turn(d_own[k]), embeds)
        last[0] = g_w[k]

    def piece_of(k):
        whole = joined[0] if isinstance(joined, list) else joined
        return whole[k * ch_dev:(k + 1) * ch_dev]

    def add_next(k):
        delta = in_turn(d_next)[:, k * ch_dev:(k + 1) * ch_dev]
        g_w[k] = (g_w[k] + grad_w_of(delta, next_rows)) * scale
        last[0] = g_w[k]

    next_ids = to_label(ids, -1)
    join(weights, 0)
    for k in range(2, n_dp):
        if k & -k == k:
            pieces[k] = in_turn(pieces[k])
            last[0] = pieces[k]
    for k in range(1, n_dp):
        join(in_turn(pieces[k]), k * ch_dev)
    joined = [in_turn(joined[0])]
    last[0] = joined[0]
    own_delta(late, piece_of(late))
    own_grad(late)
    joined = joined[0]
    next_ids = in_turn(next_ids)
    d_next = delta_of(next_rows, next_ids, joined, list(range(n_dp)))
    last[0] = d_next
    add_next(late)
    theirs = jnp.dot(in_turn(d_next), joined, preferred_element_type=jnp.float32).astype(jnp.bfloat16)
    last[0] = theirs
    back = to_label(theirs, 1)
    second = in_turn(g_w[late])
    for k in range(1, late):
        own_delta(k, piece_of(k))
        own_grad(k)
        add_next(k)

    relayed, moved = {}, {}
    moved[1] = to_dp(g_w[1].astype(jnp.bfloat16), 1)
    for h, rows in enumerate((slice(0, ch_dev // 2), slice(ch_dev // 2, ch_dev))):
        for k in range(late, 1, -1):
            step = k & -k
            part = (second if (k, h) == (late, 1) else g_w[k])[rows]
            for term in relayed.get((k, h), ()):
                part = part + in_turn(term).astype(jnp.float32)
            part = part.astype(jnp.bfloat16)
            if (k, h) in relayed:
                last[0] = part
            if step == k:
                moved[k, h] = to_dp(part, k)
            else:
                relayed.setdefault((k ^ step, h), []).append(to_dp(part, step))
    for k in range(2, n_dp):
        if (k, 0) in moved:
            moved[k, 0] = in_turn(moved[k, 0])
            last[0] = moved[k, 0]
    own_delta(0, piece_of(0))
    own_grad(0)
    grad_x = jnp.dot(
        in_turn(jnp.concatenate([d_own[k] for k in range(n_dp)], axis=1)),
        joined,
        preferred_element_type=jnp.float32,
    )
    last[0] = grad_x
    add_next(0)
    grad_w = g_w[0] + in_turn(moved[1]).astype(jnp.float32)
    for k in range(2, n_dp):
        if (k, 0) in moved:
            whole = jnp.concatenate([moved[k, 0], in_turn(moved[k, 1])], axis=0)
            grad_w = grad_w + whole.astype(jnp.float32)
    grad_w = grad_w.astype(jnp.bfloat16)
    last[0] = grad_w
    grad_x = (grad_x + in_turn(back).astype(jnp.float32)).astype(jnp.bfloat16)
    return (grad_w, grad_x)


def solution(mesh):
    return jax.shard_map(
        local,
        mesh=mesh,
        in_specs=(
            P(("groups", "label", "dp"), None),
            P(("label", "dp"), None),
            P(("groups", "label", "dp"), None),
            P(("groups", "label", "dp")),
        ),
        out_specs=(P(("groups", "label", "dp"), None), P(("groups", "label", "dp"), None)),
        check_vma=False,
    )
```

```python
import math

import jax
import jax.numpy as jnp
from jax import lax
from jax.sharding import PartitionSpec as P


def local(embeds, weights, pos_ids, pos_count):
    n_label = lax.axis_size("label")
    n_dp = lax.axis_size("dp")
    me_label = lax.axis_index("label")
    me_dp = lax.axis_index("dp")
    rows_dev, width = embeds.shape
    ch_dev = weights.shape[0]
    stretch = ch_dev * n_dp
    slots = pos_ids.shape[1]
    span = stretch * n_label // slots
    scale = 1.0 / math.sqrt(rows_dev * n_dp)
    valid = jnp.arange(slots, dtype=jnp.int32)[None, :] < pos_count[:, None]
    ids = jnp.where(valid, pos_ids, -1)
    last = [embeds]

    def in_turn(x):
        x, _ = lax.optimization_barrier((x, last[0]))
        return x

    def to_dp(x, k):
        return lax.ppermute(x, "dp", [(i, i ^ k) for i in range(n_dp)])

    def to_label(x, by):
        return lax.ppermute(x, "label", [(i, (i + by) % n_label) for i in range(n_label)])

    def delta_of(rows, row_ids, piece, ks):
        starts = [me_label * stretch + (me_dp ^ k) * ch_dev for k in ks]
        place = jnp.arange(len(ks) * ch_dev, dtype=jnp.int32)[None, :]
        for i, start in enumerate(starts):
            column = lax.dynamic_slice_in_dim(row_ids, start // span, 1, axis=1) - (start - i * ch_dev)
            sought = column if i == 0 else jnp.where(place < i * ch_dev, sought, column)
        target = (sought == place).astype(jnp.float32)
        logits = lax.dot_general(
            rows, piece, (((1,), (1,)), ((), ())), preferred_element_type=jnp.float32
        )
        return (jax.nn.sigmoid(logits) - target).astype(jnp.bfloat16)

    def grad_w_of(delta, rows):
        return lax.dot_general(
            delta, rows, (((0,), (0,)), ((), ())), preferred_element_type=jnp.float32
        )

    late = n_dp - 1
    pieces = {0: weights}
    for k in range(1, n_dp):
        step = k & -k
        pieces[k] = to_dp(pieces[k ^ step], step)
    d_own, g_w = {}, {}
    joined = [jnp.zeros((stretch, width), weights.dtype)]
    next_rows = to_label(embeds, -1)

    def join(piece, at):
        joined[0] = lax.dynamic_update_slice_in_dim(joined[0], piece, at, axis=0)

    def own_delta(k, piece):
        d_own[k] = delta_of(embeds, ids, in_turn(piece), [k])
        last[0] = d_own[k]

    def own_grad(k):
        g_w[k] = grad_w_of(in_turn(d_own[k]), embeds)
        last[0] = g_w[k]

    def piece_of(k):
        whole = joined[0] if isinstance(joined, list) else joined
        return whole[k * ch_dev:(k + 1) * ch_dev]

    def add_next(k):
        delta = in_turn(d_next)[:, k * ch_dev:(k + 1) * ch_dev]
        g_w[k] = (g_w[k] + grad_w_of(delta, next_rows)) * scale
        last[0] = g_w[k]

    next_ids = to_label(ids, -1)
    join(weights, 0)
    for k in range(2, n_dp):
        if k & -k == k:
            pieces[k] = in_turn(pieces[k])
            last[0] = pieces[k]
    for k in range(1, n_dp):
        join(in_turn(pieces[k]), k * ch_dev)
    joined = [in_turn(joined[0])]
    last[0] = joined[0]
    own_delta(late, piece_of(late))
    own_grad(late)
    joined = joined[0]
    next_ids = in_turn(next_ids)
    d_next = delta_of(next_rows, next_ids, joined, list(range(n_dp)))
    last[0] = d_next
    add_next(late)
    theirs = jnp.dot(in_turn(d_next), joined, preferred_element_type=jnp.float32).astype(jnp.bfloat16)
    last[0] = theirs
    back = to_label(theirs, 1)
    second = in_turn(g_w[late])
    for k in range(1, late):
        own_delta(k, piece_of(k))
        own_grad(k)
        add_next(k)

    relayed, moved = {}, {}
    moved[1] = to_dp(g_w[1].astype(jnp.bfloat16), 1)
    for h, rows in enumerate((slice(0, ch_dev // 2), slice(ch_dev // 2, ch_dev))):
        for k in range(late, 1, -1):
            step = k & -k
            part = (second if (k, h) == (late, 1) else g_w[k])[rows]
            for term in relayed.get((k, h), ()):
                part = part + in_turn(term).astype(jnp.float32)
            part = part.astype(jnp.bfloat16)
            if (k, h) in relayed:
                last[0] = part
            if step == k:
                moved[k, h] = to_dp(part, k)
            else:
                relayed.setdefault((k ^ step, h), []).append(to_dp(part, step))
    own_delta(0, piece_of(0))
    own_grad(0)
    grad_x = jnp.dot(
        in_turn(jnp.concatenate([d_own[k] for k in range(n_dp)], axis=1)),
        joined,
        preferred_element_type=jnp.float32,
    )
    last[0] = grad_x
    add_next(0)
    for k in range(2, n_dp):
        if (k, 0) in moved:
            moved[k, 0] = in_turn(moved[k, 0])
            last[0] = moved[k, 0]
    grad_x = (grad_x + in_turn(back).astype(jnp.float32)).astype(jnp.bfloat16)
    last[0] = grad_x
    grad_w = g_w[0] + in_turn(moved[1]).astype(jnp.float32)
    for k in range(2, n_dp):
        if (k, 0) in moved:
            whole = jnp.concatenate([moved[k, 0], in_turn(moved[k, 1])], axis=0)
            grad_w = grad_w + whole.astype(jnp.float32)
    grad_w = grad_w.astype(jnp.bfloat16)
    return (grad_w, grad_x)


def solution(mesh):
    return jax.shard_map(
        local,
        mesh=mesh,
        in_specs=(
            P(("groups", "label", "dp"), None),
            P(("label", "dp"), None),
            P(("groups", "label", "dp"), None),
            P(("groups", "label", "dp")),
        ),
        out_specs=(P(("groups", "label", "dp"), None), P(("groups", "label", "dp"), None)),
        check_vma=False,
    )
```

```python
import math

import jax
import jax.numpy as jnp
from jax import lax
from jax.sharding import PartitionSpec as P


def local(embeds, weights, pos_ids, pos_count):
    n_label = lax.axis_size("label")
    n_dp = lax.axis_size("dp")
    me_label = lax.axis_index("label")
    me_dp = lax.axis_index("dp")
    rows_dev, width = embeds.shape
    ch_dev = weights.shape[0]
    stretch = ch_dev * n_dp
    slots = pos_ids.shape[1]
    span = stretch * n_label // slots
    scale = 1.0 / math.sqrt(rows_dev * n_dp)
    valid = jnp.arange(slots, dtype=jnp.int32)[None, :] < pos_count[:, None]
    ids = jnp.where(valid, pos_ids, -1)
    last = [embeds]

    def in_turn(x):
        x, _ = lax.optimization_barrier((x, last[0]))
        return x

    def to_dp(x, k):
        return lax.ppermute(x, "dp", [(i, i ^ k) for i in range(n_dp)])

    def to_label(x, by):
        return lax.ppermute(x, "label", [(i, (i + by) % n_label) for i in range(n_label)])

    def delta_of(rows, row_ids, piece, ks):
        starts = [me_label * stretch + (me_dp ^ k) * ch_dev for k in ks]
        place = jnp.arange(len(ks) * ch_dev, dtype=jnp.int32)[None, :]
        for i, start in enumerate(starts):
            column = lax.dynamic_slice_in_dim(row_ids, start // span, 1, axis=1) - (start - i * ch_dev)
            sought = column if i == 0 else jnp.where(place < i * ch_dev, sought, column)
        target = (sought == place).astype(jnp.float32)
        logits = lax.dot_general(
            rows, piece, (((1,), (1,)), ((), ())), preferred_element_type=jnp.float32
        )
        return (jax.nn.sigmoid(logits) - target).astype(jnp.bfloat16)

    def grad_w_of(delta, rows):
        return lax.dot_general(
            delta, rows, (((0,), (0,)), ((), ())), preferred_element_type=jnp.float32
        )

    late = n_dp - 1
    pieces = {0: weights}
    for k in range(1, n_dp):
        step = k & -k
        source = pieces[k ^ step]
        if k == 1:
            source, _ = lax.optimization_barrier((source, ids))
        pieces[k] = to_dp(source, step)
    d_own, g_w = {}, {}
    joined = [jnp.zeros((stretch, width), weights.dtype)]
    next_rows = to_label(embeds, -1)

    def join(piece, at):
        joined[0] = lax.dynamic_update_slice_in_dim(joined[0], piece, at, axis=0)

    def own_delta(k, piece):
        d_own[k] = delta_of(embeds, ids, in_turn(piece), [k])
        last[0] = d_own[k]

    def own_grad(k):
        g_w[k] = grad_w_of(in_turn(d_own[k]), embeds)
        last[0] = g_w[k]

    def piece_of(k):
        whole = joined[0] if isinstance(joined, list) else joined
        return whole[k * ch_dev:(k + 1) * ch_dev]

    def add_next(k):
        delta = in_turn(d_late if k == late else d_early[:, k * ch_dev:(k + 1) * ch_dev])
        g_w[k] = (g_w[k] + grad_w_of(delta, next_rows)) * scale
        last[0] = g_w[k]

    next_ids = to_label(ids, -1)
    join(weights, 0)
    for k in range(2, n_dp):
        if k & -k == k:
            pieces[k] = in_turn(pieces[k])
            last[0] = pieces[k]
    next_rows, next_ids, pieces[1], _ = lax.optimization_barrier((next_rows, next_ids, pieces[1], last[0]))
    for k in range(1, late):
        join(pieces[k], k * ch_dev)
    early = joined[0][:late * ch_dev]
    d_early = delta_of(next_rows, next_ids, early, list(range(late)))
    last[0] = d_early
    pieces[late] = in_turn(pieces[late])
    join(pieces[late], late * ch_dev)
    joined = joined[0]
    own_delta(late, pieces[late])
    own_grad(late)
    d_late = delta_of(next_rows, next_ids, in_turn(pieces[late]), [late])
    d_next = jnp.concatenate([d_early, d_late], axis=1)
    last[0] = d_late
    add_next(late)
    theirs = jnp.dot(in_turn(d_next), joined, preferred_element_type=jnp.float32).astype(jnp.bfloat16)
    last[0] = theirs
    back = to_label(theirs, 1)
    second = in_turn(g_w[late])
    for k in range(1, late):
        own_delta(k, piece_of(k))
        own_grad(k)
        add_next(k)

    relayed, moved = {}, {}
    moved[1] = to_dp(g_w[1].astype(jnp.bfloat16), 1)
    for h, rows in enumerate((slice(0, ch_dev // 2), slice(ch_dev // 2, ch_dev))):
        for k in range(late, 1, -1):
            step = k & -k
            part = (second if (k, h) == (late, 1) else g_w[k])[rows]
            for term in relayed.get((k, h), ()):
                part = part + in_turn(term).astype(jnp.float32)
            part = part.astype(jnp.bfloat16)
            if (k, h) in relayed:
                last[0] = part
            if step == k:
                moved[k, h] = to_dp(part, k)
            else:
                relayed.setdefault((k ^ step, h), []).append(to_dp(part, step))
    own_delta(0, piece_of(0))
    own_grad(0)
    grad_x = jnp.dot(
        in_turn(jnp.concatenate([d_own[k] for k in range(n_dp)], axis=1)),
        joined,
        preferred_element_type=jnp.float32,
    )
    last[0] = grad_x
    add_next(0)
    for k in range(2, n_dp):
        if (k, 0) in moved:
            moved[k, 0] = in_turn(moved[k, 0])
            last[0] = moved[k, 0]
    grad_x = (grad_x + in_turn(back).astype(jnp.float32)).astype(jnp.bfloat16)
    last[0] = grad_x
    grad_w = g_w[0] + in_turn(moved[1]).astype(jnp.float32)
    for k in range(2, n_dp):
        if (k, 0) in moved:
            whole = jnp.concatenate([moved[k, 0], in_turn(moved[k, 1])], axis=0)
            grad_w = grad_w + whole.astype(jnp.float32)
    grad_w = grad_w.astype(jnp.bfloat16)
    return (grad_w, grad_x)


def solution(mesh):
    return jax.shard_map(
        local,
        mesh=mesh,
        in_specs=(
            P(("groups", "label", "dp"), None),
            P(("label", "dp"), None),
            P(("groups", "label", "dp"), None),
            P(("groups", "label", "dp")),
        ),
        out_specs=(P(("groups", "label", "dp"), None), P(("groups", "label", "dp"), None)),
        check_vma=False,
    )
```

```python
import math

import jax
import jax.numpy as jnp
from jax import lax
from jax.sharding import PartitionSpec as P


def local(embeds, weights, pos_ids, pos_count):
    n_groups = lax.axis_size("groups")
    n_label = lax.axis_size("label")
    n_dp = lax.axis_size("dp")
    me_group = lax.axis_index("groups")
    me_label = lax.axis_index("label")
    me_dp = lax.axis_index("dp")
    rows_dev, width = embeds.shape
    ch_dev = weights.shape[0]
    stretch = ch_dev * n_dp
    slots = pos_ids.shape[1]
    span = stretch * n_label // slots
    scale = 1.0 / math.sqrt(rows_dev * n_dp)
    valid = jnp.arange(slots, dtype=jnp.int32)[None, :] < pos_count[:, None]
    ids = jnp.where(valid, pos_ids, -1)
    last = [embeds]

    def in_turn(x):
        x, _ = lax.optimization_barrier((x, last[0]))
        return x

    def to_dp(x, k):
        return lax.ppermute(x, "dp", [(i, i ^ k) for i in range(n_dp)])

    def to_group(x):
        return lax.ppermute(x, "groups", [(i, i ^ 1) for i in range(n_groups)])

    def to_label(x, by):
        return lax.ppermute(x, "label", [(i, (i + by) % n_label) for i in range(n_label)])

    def delta_of(rows, row_ids, piece, ks):
        starts = [me_label * stretch + (me_dp ^ k) * ch_dev for k in ks]
        place = jnp.arange(len(ks) * ch_dev, dtype=jnp.int32)[None, :]
        for i, start in enumerate(starts):
            column = lax.dynamic_slice_in_dim(row_ids, start // span, 1, axis=1) - (start - i * ch_dev)
            sought = column if i == 0 else jnp.where(place < i * ch_dev, sought, column)
        target = (sought == place).astype(jnp.float32)
        logits = lax.dot_general(
            rows, piece, (((1,), (1,)), ((), ())), preferred_element_type=jnp.float32
        )
        return (jax.nn.sigmoid(logits) - target).astype(jnp.bfloat16)

    def grad_w_of(delta, rows):
        return lax.dot_general(
            delta, rows, (((0,), (0,)), ((), ())), preferred_element_type=jnp.float32
        )

    late = n_dp - 1
    half = ch_dev // 2
    mine_at, other_at = me_group * half, (1 - me_group) * half
    mine = lax.dynamic_slice_in_dim(weights, mine_at, half, axis=0)
    near_source, _ = lax.optimization_barrier((weights, ids))
    near = to_dp(near_source, 1)
    parts, others = {}, {}
    for k in range(2, n_dp):
        step = k & -k
        if step == k:
            parts[k] = to_dp(mine, k)
    d_own, g_w = {}, {}
    joined = [jnp.zeros((stretch, width), weights.dtype)]
    next_rows = to_label(embeds, -1)

    def join(piece, at):
        joined[0] = lax.dynamic_update_slice_in_dim(joined[0], piece, at, axis=0)

    def own_delta(k, piece):
        d_own[k] = delta_of(embeds, ids, in_turn(piece), [k])
        last[0] = d_own[k]

    def own_grad(k):
        g_w[k] = grad_w_of(in_turn(d_own[k]), embeds)
        last[0] = g_w[k]

    def piece_of(k):
        whole = joined[0] if isinstance(joined, list) else joined
        return whole[k * ch_dev:(k + 1) * ch_dev]

    def add_next(k):
        delta = in_turn(d_late if k == late else d_early[:, k * ch_dev:(k + 1) * ch_dev])
        g_w[k] = (g_w[k] + grad_w_of(delta, next_rows)) * scale
        last[0] = g_w[k]

    next_ids = to_label(ids, -1)
    join(weights, 0)
    for k in range(2, n_dp):
        step = k & -k
        if step < k:
            parts[k] = to_dp(parts[k ^ step], step)
        parts[k] = in_turn(parts[k])
        last[0] = parts[k]
        others[k] = to_group(parts[k])

    def join_halves(k):
        join(parts[k], k * ch_dev + mine_at)
        join(others[k], k * ch_dev + other_at)

    received = [others[k] for k in range(2, late)]
    next_rows, next_ids, near, received, _ = lax.optimization_barrier(
        (next_rows, next_ids, near, received, last[0])
    )
    join(near, ch_dev)
    for k in range(2, late):
        others[k] = received[k - 2]
        join_halves(k)
    early = joined[0][:late * ch_dev]
    d_early = delta_of(next_rows, next_ids, early, list(range(late)))
    last[0] = d_early
    others[late] = in_turn(others[late])
    join_halves(late)
    joined = joined[0]
    own_delta(late, piece_of(late))
    own_grad(late)
    d_late = delta_of(next_rows, next_ids, in_turn(piece_of(late)), [late])
    d_next = jnp.concatenate([d_early, d_late], axis=1)
    last[0] = d_late
    add_next(late)
    theirs = jnp.dot(in_turn(d_next), joined, preferred_element_type=jnp.float32).astype(jnp.bfloat16)
    last[0] = theirs
    back = to_label(theirs, 1)
    second = in_turn(g_w[late])
    for k in range(1, late):
        own_delta(k, piece_of(k))
        own_grad(k)
        add_next(k)

    relayed, moved = {}, {}
    moved[1] = to_dp(g_w[1].astype(jnp.bfloat16), 1)
    for h, rows in enumerate((slice(0, ch_dev // 2), slice(ch_dev // 2, ch_dev))):
        for k in range(late, 1, -1):
            step = k & -k
            part = (second if (k, h) == (late, 1) else g_w[k])[rows]
            for term in relayed.get((k, h), ()):
                part = part + in_turn(term).astype(jnp.float32)
            part = part.astype(jnp.bfloat16)
            if (k, h) in relayed:
                last[0] = part
            if step == k:
                moved[k, h] = to_dp(part, k)
            else:
                relayed.setdefault((k ^ step, h), []).append(to_dp(part, step))
    own_delta(0, piece_of(0))
    own_grad(0)
    grad_x = jnp.dot(
        in_turn(jnp.concatenate([d_own[k] for k in range(n_dp)], axis=1)),
        joined,
        preferred_element_type=jnp.float32,
    )
    last[0] = grad_x
    add_next(0)
    for k in range(2, n_dp):
        if (k, 0) in moved:
            moved[k, 0] = in_turn(moved[k, 0])
            last[0] = moved[k, 0]
    grad_x = (grad_x + in_turn(back).astype(jnp.float32)).astype(jnp.bfloat16)
    last[0] = grad_x
    grad_w = g_w[0] + in_turn(moved[1]).astype(jnp.float32)
    for k in range(2, n_dp):
        if (k, 0) in moved:
            whole = jnp.concatenate([moved[k, 0], in_turn(moved[k, 1])], axis=0)
            grad_w = grad_w + whole.astype(jnp.float32)
    grad_w = grad_w.astype(jnp.bfloat16)
    return (grad_w, grad_x)


def solution(mesh):
    return jax.shard_map(
        local,
        mesh=mesh,
        in_specs=(
            P(("groups", "label", "dp"), None),
            P(("label", "dp"), None),
            P(("groups", "label", "dp"), None),
            P(("groups", "label", "dp")),
        ),
        out_specs=(P(("groups", "label", "dp"), None), P(("groups", "label", "dp"), None)),
        check_vma=False,
    )
```

```python
import math

import jax
import jax.numpy as jnp
from jax import lax
from jax.sharding import PartitionSpec as P


def local(embeds, weights, pos_ids, pos_count):
    n_groups = lax.axis_size("groups")
    n_label = lax.axis_size("label")
    n_dp = lax.axis_size("dp")
    me_group = lax.axis_index("groups")
    me_label = lax.axis_index("label")
    me_dp = lax.axis_index("dp")
    rows_dev, width = embeds.shape
    ch_dev = weights.shape[0]
    stretch = ch_dev * n_dp
    slots = pos_ids.shape[1]
    span = stretch * n_label // slots
    scale = 1.0 / math.sqrt(rows_dev * n_dp)
    valid = jnp.arange(slots, dtype=jnp.int32)[None, :] < pos_count[:, None]
    ids = jnp.where(valid, pos_ids, -1)
    last = [embeds]

    def in_turn(x):
        x, _ = lax.optimization_barrier((x, last[0]))
        return x

    def to_dp(x, k):
        return lax.ppermute(x, "dp", [(i, i ^ k) for i in range(n_dp)])

    def to_group(x):
        return lax.ppermute(x, "groups", [(i, i ^ 1) for i in range(n_groups)])

    def to_label(x, by):
        return lax.ppermute(x, "label", [(i, (i + by) % n_label) for i in range(n_label)])

    def delta_of(rows, row_ids, piece, ks):
        starts = [me_label * stretch + (me_dp ^ k) * ch_dev for k in ks]
        place = jnp.arange(len(ks) * ch_dev, dtype=jnp.int32)[None, :]
        for i, start in enumerate(starts):
            column = lax.dynamic_slice_in_dim(row_ids, start // span, 1, axis=1) - (start - i * ch_dev)
            sought = column if i == 0 else jnp.where(place < i * ch_dev, sought, column)
        target = (sought == place).astype(jnp.float32)
        logits = lax.dot_general(
            rows, piece, (((1,), (1,)), ((), ())), preferred_element_type=jnp.float32
        )
        return (jax.nn.sigmoid(logits) - target).astype(jnp.bfloat16)

    def grad_w_of(delta, rows):
        return lax.dot_general(
            delta, rows, (((0,), (0,)), ((), ())), preferred_element_type=jnp.float32
        )

    late = n_dp - 1
    half = ch_dev // 2
    mine_at, other_at = me_group * half, (1 - me_group) * half
    mine = lax.dynamic_slice_in_dim(weights, mine_at, half, axis=0)
    near_source, _ = lax.optimization_barrier((weights, ids))
    near = to_dp(near_source, 1)
    parts, others = {}, {}
    for k in range(2, n_dp):
        step = k & -k
        if step == k:
            parts[k] = to_dp(mine, k)
    d_own, g_w = {}, {}
    joined = [jnp.zeros((stretch, width), weights.dtype)]
    next_rows = to_label(embeds, -1)

    def join(piece, at):
        joined[0] = lax.dynamic_update_slice_in_dim(joined[0], piece, at, axis=0)

    def own_delta(k, piece):
        d_own[k] = delta_of(embeds, ids, in_turn(piece), [k])
        last[0] = d_own[k]

    def own_grad(k):
        g_w[k] = grad_w_of(in_turn(d_own[k]), embeds)
        last[0] = g_w[k]

    def piece_of(k):
        whole = joined[0] if isinstance(joined, list) else joined
        return whole[k * ch_dev:(k + 1) * ch_dev]

    def add_next(k):
        delta = in_turn(d_late if k == late else d_early[:, k * ch_dev:(k + 1) * ch_dev])
        g_w[k] = (g_w[k] + grad_w_of(delta, next_rows)) * scale
        last[0] = g_w[k]

    next_ids = to_label(ids, -1)
    join(weights, 0)
    for k in range(2, n_dp):
        step = k & -k
        if step < k:
            parts[k] = to_dp(parts[k ^ step], step)
        parts[k] = in_turn(parts[k])
        last[0] = parts[k]
        others[k] = to_group(parts[k])

    def join_halves(k):
        join(parts[k], k * ch_dev + mine_at)
        join(others[k], k * ch_dev + other_at)

    received = [others[k] for k in range(2, late)]
    next_rows, next_ids, near, received, _ = lax.optimization_barrier(
        (next_rows, next_ids, near, received, last[0])
    )
    join(near, ch_dev)
    for k in range(2, late):
        others[k] = received[k - 2]
        join_halves(k)
    early = joined[0][:late * ch_dev]
    d_early = delta_of(next_rows, next_ids, early, list(range(late)))
    last[0] = d_early
    own_delta(1, piece_of(1))
    others[late] = in_turn(others[late])
    join_halves(late)
    joined = joined[0]
    own_delta(late, piece_of(late))
    own_grad(late)
    d_late = delta_of(next_rows, next_ids, in_turn(piece_of(late)), [late])
    d_next = jnp.concatenate([d_early, d_late], axis=1)
    last[0] = d_late
    add_next(late)
    theirs = jnp.dot(in_turn(d_next), joined, preferred_element_type=jnp.float32).astype(jnp.bfloat16)
    last[0] = theirs
    back = to_label(theirs, 1)
    second = in_turn(g_w[late])
    for k in range(1, late):
        if k > 1:
            own_delta(k, piece_of(k))
        own_grad(k)
        add_next(k)

    relayed, moved = {}, {}
    moved[1] = to_dp(g_w[1].astype(jnp.bfloat16), 1)
    for h, rows in enumerate((slice(0, ch_dev // 2), slice(ch_dev // 2, ch_dev))):
        for k in range(late, 1, -1):
            step = k & -k
            part = (second if (k, h) == (late, 1) else g_w[k])[rows]
            for term in relayed.get((k, h), ()):
                part = part + in_turn(term).astype(jnp.float32)
            part = part.astype(jnp.bfloat16)
            if (k, h) in relayed:
                last[0] = part
            if step == k:
                moved[k, h] = to_dp(part, k)
            else:
                relayed.setdefault((k ^ step, h), []).append(to_dp(part, step))
    own_delta(0, piece_of(0))
    own_grad(0)
    grad_x = jnp.dot(
        in_turn(jnp.concatenate([d_own[k] for k in range(n_dp)], axis=1)),
        joined,
        preferred_element_type=jnp.float32,
    )
    last[0] = grad_x
    add_next(0)
    for k in range(2, n_dp):
        if (k, 0) in moved:
            moved[k, 0] = in_turn(moved[k, 0])
            last[0] = moved[k, 0]
    grad_x = (grad_x + in_turn(back).astype(jnp.float32)).astype(jnp.bfloat16)
    last[0] = grad_x
    grad_w = g_w[0] + in_turn(moved[1]).astype(jnp.float32)
    for k in range(2, n_dp):
        if (k, 0) in moved:
            whole = jnp.concatenate([moved[k, 0], in_turn(moved[k, 1])], axis=0)
            grad_w = grad_w + whole.astype(jnp.float32)
    grad_w = grad_w.astype(jnp.bfloat16)
    return (grad_w, grad_x)


def solution(mesh):
    return jax.shard_map(
        local,
        mesh=mesh,
        in_specs=(
            P(("groups", "label", "dp"), None),
            P(("label", "dp"), None),
            P(("groups", "label", "dp"), None),
            P(("groups", "label", "dp")),
        ),
        out_specs=(P(("groups", "label", "dp"), None), P(("groups", "label", "dp"), None)),
        check_vma=False,
    )
```

```python
import math

import jax
import jax.numpy as jnp
from jax import lax
from jax.sharding import PartitionSpec as P


def local(embeds, weights, pos_ids, pos_count):
    n_groups = lax.axis_size("groups")
    n_label = lax.axis_size("label")
    n_dp = lax.axis_size("dp")
    me_group = lax.axis_index("groups")
    me_label = lax.axis_index("label")
    me_dp = lax.axis_index("dp")
    rows_dev, width = embeds.shape
    ch_dev = weights.shape[0]
    stretch = ch_dev * n_dp
    slots = pos_ids.shape[1]
    span = stretch * n_label // slots
    scale = 1.0 / math.sqrt(rows_dev * n_dp)
    valid = jnp.arange(slots, dtype=jnp.int32)[None, :] < pos_count[:, None]
    ids = jnp.where(valid, pos_ids, -1)
    last = [embeds]

    def in_turn(x):
        x, _ = lax.optimization_barrier((x, last[0]))
        return x

    def to_dp(x, k):
        return lax.ppermute(x, "dp", [(i, i ^ k) for i in range(n_dp)])

    def to_group(x):
        return lax.ppermute(x, "groups", [(i, i ^ 1) for i in range(n_groups)])

    def to_label(x, by):
        return lax.ppermute(x, "label", [(i, (i + by) % n_label) for i in range(n_label)])

    def delta_of(rows, row_ids, piece, ks):
        starts = [me_label * stretch + (me_dp ^ k) * ch_dev for k in ks]
        place = jnp.arange(len(ks) * ch_dev, dtype=jnp.int32)[None, :]
        for i, start in enumerate(starts):
            column = lax.dynamic_slice_in_dim(row_ids, start // span, 1, axis=1) - (start - i * ch_dev)
            sought = column if i == 0 else jnp.where(place < i * ch_dev, sought, column)
        target = (sought == place).astype(jnp.float32)
        logits = lax.dot_general(
            rows, piece, (((1,), (1,)), ((), ())), preferred_element_type=jnp.float32
        )
        return (jax.nn.sigmoid(logits) - target).astype(jnp.bfloat16)

    def grad_w_of(delta, rows):
        return lax.dot_general(
            delta, rows, (((0,), (0,)), ((), ())), preferred_element_type=jnp.float32
        )

    late = n_dp - 1
    half = ch_dev // 2
    mine_at, other_at = me_group * half, (1 - me_group) * half
    mine = lax.dynamic_slice_in_dim(weights, mine_at, half, axis=0)
    near = to_dp(weights, 1)
    parts, others = {}, {}
    for k in range(2, n_dp):
        step = k & -k
        if step == k:
            parts[k] = to_dp(mine, k)
    d_own, g_w = {}, {}
    joined = [jnp.zeros((stretch, width), weights.dtype)]
    next_rows = to_label(embeds, -1)

    def join(piece, at):
        joined[0] = lax.dynamic_update_slice_in_dim(joined[0], piece, at, axis=0)

    def own_delta(k, piece):
        d_own[k] = delta_of(embeds, ids, in_turn(piece), [k])
        last[0] = d_own[k]

    def own_grad(k):
        g_w[k] = grad_w_of(in_turn(d_own[k]), embeds)
        last[0] = g_w[k]

    def piece_of(k):
        whole = joined[0] if isinstance(joined, list) else joined
        return whole[k * ch_dev:(k + 1) * ch_dev]

    def add_next(k):
        delta = in_turn(d_late if k == late else d_early[:, k * ch_dev:(k + 1) * ch_dev])
        g_w[k] = (g_w[k] + grad_w_of(delta, next_rows)) * scale
        last[0] = g_w[k]

    next_ids = to_label(ids, -1)
    join(weights, 0)
    for k in range(2, n_dp):
        step = k & -k
        if step < k:
            parts[k] = to_dp(parts[k ^ step], step)
        parts[k] = in_turn(parts[k])
        last[0] = parts[k]
        others[k] = to_group(parts[k])

    def join_halves(k):
        join(parts[k], k * ch_dev + mine_at)
        join(others[k], k * ch_dev + other_at)

    received = [others[k] for k in range(2, late)]
    next_rows, next_ids, near, received, _ = lax.optimization_barrier(
        (next_rows, next_ids, near, received, last[0])
    )
    join(near, ch_dev)
    for k in range(2, late):
        others[k] = received[k - 2]
        join_halves(k)
    early = joined[0][:late * ch_dev]
    d_early = delta_of(next_rows, next_ids, early, list(range(late)))
    last[0] = d_early
    own_delta(1, piece_of(1))
    others[late] = in_turn(others[late])
    join_halves(late)
    joined = joined[0]
    own_delta(late, piece_of(late))
    own_grad(late)
    d_late = delta_of(next_rows, next_ids, in_turn(piece_of(late)), [late])
    d_next = jnp.concatenate([d_early, d_late], axis=1)
    last[0] = d_late
    add_next(late)
    theirs = jnp.dot(in_turn(d_next), joined, preferred_element_type=jnp.float32).astype(jnp.bfloat16)
    last[0] = theirs
    back = to_label(theirs, 1)
    second = in_turn(g_w[late])
    for k in range(1, late):
        if k > 1:
            own_delta(k, piece_of(k))
        own_grad(k)
        add_next(k)

    relayed, moved = {}, {}
    moved[1] = to_dp(g_w[1].astype(jnp.bfloat16), 1)
    for h, rows in enumerate((slice(0, ch_dev // 2), slice(ch_dev // 2, ch_dev))):
        for k in range(late, 1, -1):
            step = k & -k
            part = (second if (k, h) == (late, 1) else g_w[k])[rows]
            for term in relayed.get((k, h), ()):
                part = part + in_turn(term).astype(jnp.float32)
            part = part.astype(jnp.bfloat16)
            if (k, h) in relayed:
                last[0] = part
            if step == k:
                moved[k, h] = to_dp(part, k)
            else:
                relayed.setdefault((k ^ step, h), []).append(to_dp(part, step))
    own_delta(0, piece_of(0))
    own_grad(0)
    grad_x = jnp.dot(
        in_turn(jnp.concatenate([d_own[k] for k in range(n_dp)], axis=1)),
        joined,
        preferred_element_type=jnp.float32,
    )
    last[0] = grad_x
    add_next(0)
    for k in range(2, n_dp):
        if (k, 0) in moved:
            moved[k, 0] = in_turn(moved[k, 0])
            last[0] = moved[k, 0]
    grad_x = (grad_x + in_turn(back).astype(jnp.float32)).astype(jnp.bfloat16)
    last[0] = grad_x
    grad_w = g_w[0] + in_turn(moved[1]).astype(jnp.float32)
    for k in range(2, n_dp):
        if (k, 0) in moved:
            whole = jnp.concatenate([moved[k, 0], in_turn(moved[k, 1])], axis=0)
            grad_w = grad_w + whole.astype(jnp.float32)
    grad_w = grad_w.astype(jnp.bfloat16)
    return (grad_w, grad_x)


def solution(mesh):
    return jax.shard_map(
        local,
        mesh=mesh,
        in_specs=(
            P(("groups", "label", "dp"), None),
            P(("label", "dp"), None),
            P(("groups", "label", "dp"), None),
            P(("groups", "label", "dp")),
        ),
        out_specs=(P(("groups", "label", "dp"), None), P(("groups", "label", "dp"), None)),
        check_vma=False,
    )
```

```python
import math

import jax
import jax.numpy as jnp
from jax import lax
from jax.sharding import PartitionSpec as P


def local(embeds, weights, pos_ids, pos_count):
    n_groups = lax.axis_size("groups")
    n_label = lax.axis_size("label")
    n_dp = lax.axis_size("dp")
    me_group = lax.axis_index("groups")
    me_label = lax.axis_index("label")
    me_dp = lax.axis_index("dp")
    rows_dev, width = embeds.shape
    ch_dev = weights.shape[0]
    stretch = ch_dev * n_dp
    slots = pos_ids.shape[1]
    span = stretch * n_label // slots
    scale = 1.0 / math.sqrt(rows_dev * n_dp)
    valid = jnp.arange(slots, dtype=jnp.int32)[None, :] < pos_count[:, None]
    ids = jnp.where(valid, pos_ids, -1)
    last = [embeds]

    def in_turn(x):
        x, _ = lax.optimization_barrier((x, last[0]))
        return x

    def to_dp(x, k):
        return lax.ppermute(x, "dp", [(i, i ^ k) for i in range(n_dp)])

    def to_group(x):
        return lax.ppermute(x, "groups", [(i, i ^ 1) for i in range(n_groups)])

    def to_label(x, by):
        return lax.ppermute(x, "label", [(i, (i + by) % n_label) for i in range(n_label)])

    def delta_of(rows, row_ids, piece, ks):
        starts = [me_label * stretch + (me_dp ^ k) * ch_dev for k in ks]
        place = jnp.arange(len(ks) * ch_dev, dtype=jnp.int32)[None, :]
        for i, start in enumerate(starts):
            column = lax.dynamic_slice_in_dim(row_ids, start // span, 1, axis=1) - (start - i * ch_dev)
            sought = column if i == 0 else jnp.where(place < i * ch_dev, sought, column)
        target = (sought == place).astype(jnp.float32)
        logits = lax.dot_general(
            rows, piece, (((1,), (1,)), ((), ())), preferred_element_type=jnp.float32
        )
        return (jax.nn.sigmoid(logits) - target).astype(jnp.bfloat16)

    def grad_w_of(delta, rows):
        return lax.dot_general(
            delta, rows, (((0,), (0,)), ((), ())), preferred_element_type=jnp.float32
        )

    late = n_dp - 1
    half = ch_dev // 2
    mine_at, other_at = me_group * half, (1 - me_group) * half
    mine = lax.dynamic_slice_in_dim(weights, mine_at, half, axis=0)
    near = to_dp(weights, 1)
    parts, others = {}, {}
    for k in range(2, n_dp):
        step = k & -k
        if step == k:
            parts[k] = to_dp(mine, k)
    d_own, g_w = {}, {}
    joined = [jnp.zeros((stretch, width), weights.dtype)]
    next_rows = to_label(embeds, -1)

    def join(piece, at):
        joined[0] = lax.dynamic_update_slice_in_dim(joined[0], piece, at, axis=0)

    def own_delta(k, piece):
        d_own[k] = delta_of(embeds, ids, in_turn(piece), [k])
        last[0] = d_own[k]

    def own_grad(k):
        g_w[k] = grad_w_of(in_turn(d_own[k]), embeds)
        last[0] = g_w[k]

    def piece_of(k):
        whole = joined[0] if isinstance(joined, list) else joined
        return whole[k * ch_dev:(k + 1) * ch_dev]

    def add_next(k):
        delta = in_turn(d_late if k == late else d_early[:, k * ch_dev:(k + 1) * ch_dev])
        g_w[k] = (g_w[k] + grad_w_of(delta, next_rows)) * scale
        last[0] = g_w[k]

    next_ids = to_label(ids, -1)
    join(weights, 0)
    for k in range(2, n_dp):
        step = k & -k
        if step < k:
            parts[k] = to_dp(parts[k ^ step], step)
        parts[k] = in_turn(parts[k])
        last[0] = parts[k]
        others[k] = to_group(parts[k])

    def join_halves(k):
        join(parts[k], k * ch_dev + mine_at)
        join(others[k], k * ch_dev + other_at)

    received = [others[k] for k in range(2, late)]
    next_rows, next_ids, near, received, _ = lax.optimization_barrier(
        (next_rows, next_ids, near, received, last[0])
    )
    join(near, ch_dev)
    for k in range(2, late):
        others[k] = received[k - 2]
        join_halves(k)
    early = joined[0][:late * ch_dev]
    d_early = delta_of(next_rows, next_ids, early, list(range(late)))
    last[0] = d_early
    own_delta(1, piece_of(1))
    others[late] = in_turn(others[late])
    join_halves(late)
    joined = joined[0]
    own_delta(late, piece_of(late))
    own_grad(late)
    d_late = delta_of(next_rows, next_ids, in_turn(piece_of(late)), [late])
    d_next = jnp.concatenate([d_early, d_late], axis=1)
    last[0] = d_late
    add_next(late)
    second = in_turn(g_w[late])
    theirs = jnp.dot(in_turn(d_next), joined, preferred_element_type=jnp.float32).astype(jnp.bfloat16)
    last[0] = theirs
    back = to_label(theirs, 1)
    for k in range(1, late):
        if k > 1:
            own_delta(k, piece_of(k))
        own_grad(k)
        add_next(k)

    relayed, moved = {}, {}
    moved[1] = to_dp(g_w[1].astype(jnp.bfloat16), 1)
    for h, rows in enumerate((slice(0, ch_dev // 2), slice(ch_dev // 2, ch_dev))):
        for k in range(late, 1, -1):
            step = k & -k
            part = (second if (k, h) == (late, 1) else g_w[k])[rows]
            for term in relayed.get((k, h), ()):
                part = part + in_turn(term).astype(jnp.float32)
            part = part.astype(jnp.bfloat16)
            if (k, h) in relayed:
                last[0] = part
            if step == k:
                moved[k, h] = to_dp(part, k)
            else:
                relayed.setdefault((k ^ step, h), []).append(to_dp(part, step))
    own_delta(0, piece_of(0))
    own_grad(0)
    grad_x = jnp.dot(
        in_turn(jnp.concatenate([d_own[k] for k in range(n_dp)], axis=1)),
        joined,
        preferred_element_type=jnp.float32,
    )
    last[0] = grad_x
    add_next(0)
    for k in range(2, n_dp):
        if (k, 0) in moved:
            moved[k, 0] = in_turn(moved[k, 0])
            last[0] = moved[k, 0]
    grad_x = (grad_x + in_turn(back).astype(jnp.float32)).astype(jnp.bfloat16)
    last[0] = grad_x
    grad_w = g_w[0] + in_turn(moved[1]).astype(jnp.float32)
    for k in range(2, n_dp):
        if (k, 0) in moved:
            whole = jnp.concatenate([moved[k, 0], in_turn(moved[k, 1])], axis=0)
            grad_w = grad_w + whole.astype(jnp.float32)
    grad_w = grad_w.astype(jnp.bfloat16)
    return (grad_w, grad_x)


def solution(mesh):
    return jax.shard_map(
        local,
        mesh=mesh,
        in_specs=(
            P(("groups", "label", "dp"), None),
            P(("label", "dp"), None),
            P(("groups", "label", "dp"), None),
            P(("groups", "label", "dp")),
        ),
        out_specs=(P(("groups", "label", "dp"), None), P(("groups", "label", "dp"), None)),
        check_vma=False,
    )
```

```python
import math

import jax
import jax.numpy as jnp
from jax import lax
from jax.sharding import PartitionSpec as P


def local(embeds, weights, pos_ids, pos_count):
    n_groups = lax.axis_size("groups")
    n_label = lax.axis_size("label")
    n_dp = lax.axis_size("dp")
    me_group = lax.axis_index("groups")
    me_label = lax.axis_index("label")
    me_dp = lax.axis_index("dp")
    rows_dev, width = embeds.shape
    ch_dev = weights.shape[0]
    stretch = ch_dev * n_dp
    slots = pos_ids.shape[1]
    span = stretch * n_label // slots
    scale = 1.0 / math.sqrt(rows_dev * n_dp)
    valid = jnp.arange(slots, dtype=jnp.int32)[None, :] < pos_count[:, None]
    ids = jnp.where(valid, pos_ids, -1)
    last = [embeds]

    def in_turn(x):
        x, _ = lax.optimization_barrier((x, last[0]))
        return x

    def to_dp(x, k):
        return lax.ppermute(x, "dp", [(i, i ^ k) for i in range(n_dp)])

    def to_group(x):
        return lax.ppermute(x, "groups", [(i, i ^ 1) for i in range(n_groups)])

    def to_label(x, by):
        return lax.ppermute(x, "label", [(i, (i + by) % n_label) for i in range(n_label)])

    def delta_of(rows, row_ids, piece, ks):
        starts = [me_label * stretch + (me_dp ^ k) * ch_dev for k in ks]
        place = jnp.arange(len(ks) * ch_dev, dtype=jnp.int32)[None, :]
        for i, start in enumerate(starts):
            column = lax.dynamic_slice_in_dim(row_ids, start // span, 1, axis=1) - (start - i * ch_dev)
            sought = column if i == 0 else jnp.where(place < i * ch_dev, sought, column)
        target = (sought == place).astype(jnp.float32)
        logits = lax.dot_general(
            rows, piece, (((1,), (1,)), ((), ())), preferred_element_type=jnp.float32
        )
        return (jax.nn.sigmoid(logits) - target).astype(jnp.bfloat16)

    def grad_w_of(delta, rows):
        return lax.dot_general(
            delta, rows, (((0,), (0,)), ((), ())), preferred_element_type=jnp.float32
        )

    late = n_dp - 1
    half = ch_dev // 2
    mine_at, other_at = me_group * half, (1 - me_group) * half
    mine = lax.dynamic_slice_in_dim(weights, mine_at, half, axis=0)
    near = to_dp(weights, 1)
    parts, others = {}, {}
    for k in range(2, n_dp):
        step = k & -k
        if step == k:
            parts[k] = to_dp(mine, k)
    d_own, g_w = {}, {}
    joined = [jnp.zeros((stretch, width), weights.dtype)]
    next_rows = to_label(embeds, -1)

    def join(piece, at):
        joined[0] = lax.dynamic_update_slice_in_dim(joined[0], piece, at, axis=0)

    def own_delta(k, piece):
        d_own[k] = delta_of(embeds, ids, in_turn(piece), [k])
        last[0] = d_own[k]

    def own_grad(k):
        g_w[k] = grad_w_of(in_turn(d_own[k]), embeds)
        last[0] = g_w[k]

    def piece_of(k):
        whole = joined[0] if isinstance(joined, list) else joined
        return whole[k * ch_dev:(k + 1) * ch_dev]

    def add_next(k):
        delta = in_turn(d_late if k == late else d_early[:, k * ch_dev:(k + 1) * ch_dev])
        g_w[k] = (g_w[k] + grad_w_of(delta, next_rows)) * scale
        last[0] = g_w[k]

    next_ids = to_label(ids, -1)
    join(weights, 0)
    for k in range(2, n_dp):
        step = k & -k
        if step < k:
            parts[k] = to_dp(parts[k ^ step], step)
        parts[k] = in_turn(parts[k])
        last[0] = parts[k]
        others[k] = to_group(parts[k])

    def join_halves(k):
        join(parts[k], k * ch_dev + mine_at)
        join(others[k], k * ch_dev + other_at)

    received = [others[k] for k in range(2, late)]
    next_rows, next_ids, near, received, _ = lax.optimization_barrier(
        (next_rows, next_ids, near, received, last[0])
    )
    join(near, ch_dev)
    for k in range(2, late):
        others[k] = received[k - 2]
        join_halves(k)
    early = joined[0][:late * ch_dev]
    d_early = delta_of(next_rows, next_ids, early, list(range(late)))
    last[0] = d_early
    own_delta(1, piece_of(1))
    others[late] = in_turn(others[late])
    join_halves(late)
    joined = joined[0]
    own_delta(late, piece_of(late))
    own_grad(late)
    d_late = delta_of(next_rows, next_ids, in_turn(piece_of(late)), [late])
    d_next = jnp.concatenate([d_early, d_late], axis=1)
    last[0] = d_late
    add_next(late)
    second = in_turn(g_w[late])
    theirs = jnp.dot(in_turn(d_next), joined, preferred_element_type=jnp.float32).astype(jnp.bfloat16)
    last[0] = theirs
    back = to_label(theirs, 1)
    for k in range(1, late):
        if k > 1:
            own_delta(k, piece_of(k))
        own_grad(k)
        add_next(k)

    relayed, moved = {}, {}
    moved[1] = to_dp(g_w[1].astype(jnp.bfloat16), 1)
    for h, rows in enumerate((slice(0, ch_dev // 2), slice(ch_dev // 2, ch_dev))):
        for k in range(late, 1, -1):
            step = k & -k
            part = (second if (k, h) == (late, 1) else g_w[k])[rows]
            for term in relayed.get((k, h), ()):
                part = part + in_turn(term).astype(jnp.float32)
            part = part.astype(jnp.bfloat16)
            if (k, h) in relayed:
                last[0] = part
            if step == k:
                moved[k, h] = to_dp(part, k)
            else:
                relayed.setdefault((k ^ step, h), []).append(to_dp(part, step))
    own_delta(0, piece_of(0))
    own_grad(0)
    grad_x = jnp.dot(
        in_turn(jnp.concatenate([d_own[k] for k in range(n_dp)], axis=1)),
        joined,
        preferred_element_type=jnp.float32,
    ).astype(jnp.bfloat16)
    last[0] = grad_x
    add_next(0)
    for k in range(2, n_dp):
        if (k, 0) in moved:
            moved[k, 0] = in_turn(moved[k, 0])
            last[0] = moved[k, 0]
    grad_x = (grad_x.astype(jnp.float32) + in_turn(back).astype(jnp.float32)).astype(jnp.bfloat16)
    last[0] = grad_x
    grad_w = g_w[0] + in_turn(moved[1]).astype(jnp.float32)
    for k in range(2, n_dp):
        if (k, 0) in moved:
            whole = jnp.concatenate([moved[k, 0], in_turn(moved[k, 1])], axis=0)
            grad_w = grad_w + whole.astype(jnp.float32)
    grad_w = grad_w.astype(jnp.bfloat16)
    return (grad_w, grad_x)


def solution(mesh):
    return jax.shard_map(
        local,
        mesh=mesh,
        in_specs=(
            P(("groups", "label", "dp"), None),
            P(("label", "dp"), None),
            P(("groups", "label", "dp"), None),
            P(("groups", "label", "dp")),
        ),
        out_specs=(P(("groups", "label", "dp"), None), P(("groups", "label", "dp"), None)),
        check_vma=False,
    )
```
